128 devices in a mesh: tm: 64 (over x, z, y_lo, core), height: 2 (over y_hi).
Axes of the slice: x: 4, y: 4 (y_hi: 2, y_lo: 2; y = y_hi * 2 + y_lo), z: 4, core: 2. Of those that a mesh axis runs over, the one named last changes fastest.
Arguments:
- latents: bfloat16 [256, 4, 128, 320], P('tm', 'height'), may hold values from -6 to 6
- levels: int32 [256], P('tm'), may hold values from 0 to 999
- conv_first: bfloat16 [3, 3, 320, 320], replicated, may hold values from -0.109375 to 0.109375
- emb_weight: bfloat16 [320, 320], replicated, may hold values from -0.625 to 0.625
- conv_second: bfloat16 [3, 3, 320, 320], replicated, may hold values from -0.109375 to 0.109375
- ln_gain: float32 [320], replicated, may hold values from 0.1 to 1.9
- w_query: bfloat16 [320, 320], replicated, may hold values from -0.3125 to 0.3125
- w_key: bfloat16 [320, 320], replicated, may hold values from -0.3125 to 0.3125
- w_value: bfloat16 [320, 320], replicated, may hold values from -0.3125 to 0.3125
- w_out: bfloat16 [320, 320], replicated, may hold values from -0.3125 to 0.3125
Outputs:
- mixed: bfloat16 [256, 4, 128, 320], P('tm', 'height')
The draws below stay inside these ranges and needn't reach their ends.
All inputs are finite; a program needn't handle non-finite values.
Results may differ from the reference program's by a relative error of at most 0.012.
Values may be sent and summed in bfloat16 or wider, within the bound.
No kernel may reach another device: no remote copies, remote signals or barrier semaphores. Data moves between devices by JAX's collectives and lax.ppermute only.
A program may use at most 128 MiB of HBM per device.

```python
import math
import jax
import jax.numpy as jnp
from jax import lax

C = 320
HEADS = 5
GROUPS = 32
W = 128
WINDOW = 16
LEVELS = 1000
FRAMES = 256
ROWS = 4


def place_ends(array, stream_key, smallest, largest):
    dims = array.shape
    index_at = [jax.random.randint(jax.random.fold_in(stream_key, axis), (), 0, dims[axis]) for axis in range(len(dims))]
    array = array.at[tuple(index_at)].set(smallest)
    longest = dims.index(max(dims))
    index_at[longest] = (index_at[longest] + 1) % dims[longest]
    return array.at[tuple(index_at)].set(largest)


def block_scale(stream_key, extent, cuts, smallest, largest):
    def one(axis_at, blocks):
        steps = jax.random.uniform(jax.random.fold_in(jax.random.fold_in(stream_key, 6), axis_at), (blocks,), jnp.float32, smallest / len(cuts), largest / len(cuts))
        return jnp.repeat(jnp.exp(steps), extent[axis_at] // blocks).reshape((-1,) + (1,) * (len(extent) - axis_at - 1))

    loudness = one(*cuts[0])
    for cut in cuts[1:]:
        loudness = loudness * one(*cut)
    return loudness


def bell_draw(rng, shape, spread, bound, cuts=(), kind=jnp.bfloat16):
    drawn = jax.random.normal(rng, shape, jnp.float32) * spread
    if len(cuts) > 0:
        drawn = block_scale(rng, shape, cuts, -0.22, 0.18) * drawn
    return jnp.clip(drawn, min=-bound, max=bound).astype(kind)


def setup_inputs(seed: int = 0) -> dict:
    splits = jax.random.split(jax.random.key(seed), 11)
    return {
        "latents": bell_draw(splits[0], (FRAMES, ROWS, W, C), 1.0, 6.0, ((0, 64), (1, 2))),
        "levels": place_ends(jax.random.randint(splits[1], (FRAMES,), 0, LEVELS), jax.random.fold_in(splits[1], 1), 0, LEVELS - 1).astype(jnp.int32),
        "conv_first": bell_draw(splits[2], (3, 3, C, C), (9 * C) ** -0.5, 0.109375),
        "emb_weight": bell_draw(splits[3], (C, C), (C // 4) ** -0.5, 0.625),
        "conv_second": bell_draw(splits[4], (3, 3, C, C), (9 * C) ** -0.5, 0.109375),
        "ln_gain": jnp.clip(1.0 + 0.18 * jax.random.normal(splits[5], (C,), jnp.float32), 0.1, 1.9),
        "w_query": bell_draw(splits[6], (C, C), C ** -0.5, 0.3125),
        "w_key": bell_draw(splits[7], (C, C), C ** -0.5, 0.3125),
        "w_value": bell_draw(splits[8], (C, C), C ** -0.5, 0.3125),
        "w_out": bell_draw(splits[9], (C, C), C ** -0.5, 0.3125),
    }


def norm_silu(hidden):
    frames, rows_all, columns, chans = hidden.shape
    grouped = hidden.reshape(frames, rows_all * columns, GROUPS, chans // GROUPS)
    totals = lax.optimization_barrier(jnp.sum(grouped, axis=(1, 3)))
    squares = lax.optimization_barrier(jnp.sum(grouped * grouped, axis=(1, 3)))
    count = rows_all * columns * (chans // GROUPS)
    mean = totals / count
    var = squares / count - mean * mean
    scaled = (grouped - mean[:, None, :, None]) * lax.rsqrt(var + 1e-05)[:, None, :, None]
    return jax.nn.silu(scaled).reshape(hidden.shape).astype(jnp.bfloat16)

def conv_taps(padded, weight):
    frames, rows_pad, columns, chans = padded.shape
    rows_in = rows_pad - 2
    wide = jnp.pad(padded, ((0, 0), (0, 0), (1, 1), (0, 0)))
    total = jnp.zeros((frames * rows_in * columns, weight.shape[3]), jnp.float32)
    for dy in range(3):
        for dx in range(3):
            piece = wide[:, dy:dy + rows_in, dx:dx + columns, :].reshape(-1, chans)
            total = total + jnp.dot(piece, weight[dy, dx], preferred_element_type=jnp.float32)
    return total.reshape(frames, rows_in, columns, weight.shape[3])

def level_embedding(levels, emb_weight):
    half = emb_weight.shape[0] // 2
    freqs = jnp.exp(-math.log(10000.0) * jnp.arange(half).astype(jnp.float32) / half)
    angles = levels.astype(jnp.float32)[:, None] * freqs[None, :]
    sinus = jnp.concatenate([jnp.cos(angles), jnp.sin(angles)], axis=1)
    return jnp.dot(jax.nn.silu(sinus).astype(jnp.bfloat16), emb_weight, preferred_element_type=jnp.float32)

def layer_norm(flat, ln_gain):
    values = flat.astype(jnp.float32)
    mean = lax.optimization_barrier(jnp.mean(values, axis=-1, keepdims=True))
    var = lax.optimization_barrier(jnp.mean((values - mean) ** 2, axis=-1, keepdims=True))
    return ((values - mean) * lax.rsqrt(var + 1e-05) * ln_gain).astype(jnp.bfloat16)

def project(normed, weight):
    shape = normed.shape
    out = jnp.dot(normed.reshape(-1, shape[-1]), weight, preferred_element_type=jnp.float32)
    return out.astype(jnp.bfloat16).reshape(shape[:-1] + (weight.shape[1],))

def reference(latents, levels, conv_first, emb_weight, conv_second, ln_gain, w_query, w_key, w_value, w_out):
    hidden = latents.astype(jnp.float32)
    act_first = norm_silu(hidden)
    pad_rows = ((0, 0), (1, 1), (0, 0), (0, 0))
    inner = conv_taps(jnp.pad(act_first, pad_rows), conv_first) + level_embedding(levels, emb_weight)[:, None, None, :]
    act_second = norm_silu(inner)
    resout = (hidden + conv_taps(jnp.pad(act_second, pad_rows), conv_second)).astype(jnp.bfloat16)
    frames, rows_all, columns, chans = resout.shape
    cells = rows_all * columns
    flat = resout.reshape(frames, cells, chans)
    normed = layer_norm(flat, ln_gain)
    query = project(normed, w_query)
    keys = project(normed, w_key)
    values = project(normed, w_value)
    head_size = chans // HEADS
    back = WINDOW // 2
    ahead = WINDOW // 2 - 1
    query_f = query.astype(jnp.float32).reshape(frames, cells, HEADS, head_size)
    key_pad = jnp.pad(keys, ((back, ahead), (0, 0), (0, 0)))
    value_pad = jnp.pad(values, ((back, ahead), (0, 0), (0, 0)))
    frame_ids = jnp.arange(frames)
    weights = []
    for offset in range(-back, ahead + 1):
        shifted = key_pad[back + offset:back + offset + frames].astype(jnp.float32).reshape(frames, cells, HEADS, head_size)
        score = lax.optimization_barrier(jnp.sum(query_f * shifted, axis=-1)) / math.sqrt(head_size)
        valid = (frame_ids + offset >= 0) & (frame_ids + offset < frames)
        weights.append(jnp.where(valid[:, None, None], jnp.exp(score), 0.0))
    denom = weights[0]
    for extra in weights[1:]:
        denom = denom + extra
    attended = jnp.zeros((frames, cells, HEADS, head_size), jnp.float32)
    for index, offset in enumerate(range(-back, ahead + 1)):
        probs = (weights[index] / denom).astype(jnp.bfloat16)
        shifted = value_pad[back + offset:back + offset + frames].astype(jnp.float32).reshape(frames, cells, HEADS, head_size)
        attended = attended + probs.astype(jnp.float32)[..., None] * shifted
    attended = attended.astype(jnp.bfloat16).reshape(frames * cells, chans)
    mixed = flat.astype(jnp.float32).reshape(frames * cells, chans) + jnp.dot(attended, w_out, preferred_element_type=jnp.float32)
    return mixed.astype(jnp.bfloat16).reshape(frames, rows_all, columns, chans)
```

```python
import functools
import math

import jax
import jax.numpy as jnp
from jax import lax
from jax.experimental import pallas as pl
from jax.experimental.pallas import tpu as pltpu
from jax.sharding import PartitionSpec as P

HEADS = 5
GROUPS = 32
WINDOW = 16
C = 320
MAIN = 256
TAIL = C - MAIN
COLS = 128
CELLS = 512
AXES = ("tm", "height")
F32 = jnp.float32
BF16 = jnp.bfloat16


def dot32(a, b):
    return jnp.dot(a, b, preferred_element_type=F32)


def pack_conv(weight):
    by_input = jnp.transpose(weight, (1, 2, 0, 3))
    columns = jnp.concatenate(
        [
            by_input[..., :MAIN].reshape(3, C, 3 * MAIN),
            by_input[..., MAIN:].reshape(3, C, 3 * TAIL),
        ],
        axis=2,
    )
    rows = [columns[:, :MAIN].reshape(3 * MAIN, 3 * C), columns[:, MAIN:].reshape(3 * TAIL, 3 * C)]
    return jnp.concatenate(rows + [jnp.zeros((TAIL, 3 * C), weight.dtype)], axis=0)


def level_embedding(levels, emb_weight):
    half = emb_weight.shape[0] // 2
    freqs = jnp.exp(-math.log(10000.0) * jnp.arange(half).astype(jnp.float32) / half)
    angles = levels.astype(jnp.float32)[:, None] * freqs[None, :]
    sinus = jnp.concatenate([jnp.cos(angles), jnp.sin(angles)], axis=1)
    return jnp.dot(
        jax.nn.silu(sinus).astype(jnp.bfloat16), emb_weight, preferred_element_type=jnp.float32
    )


def split3(row):
    first = row.astype(BF16)
    rest = row - first.astype(F32)
    second = rest.astype(BF16)
    return [first, second, (rest - second.astype(F32)).astype(BF16)]


def group_scale(main, tail, group_map):
    parts = []
    for value in (main, tail):
        total = jnp.sum(value, axis=0, keepdims=True)
        square = jnp.sum(value * value, axis=0, keepdims=True)
        rows = split3(total) + split3(square)
        rows = [r.astype(F32) for r in rows] + [jnp.zeros_like(total)] * 2
        parts.append(jnp.concatenate(rows, axis=0).astype(BF16))
    sums = dot32(parts[0], group_map[:MAIN, :]) + dot32(parts[1], group_map[MAIN:, :])
    count = CELLS * (C // GROUPS)
    mean = (sums[0:1] + sums[1:2] + sums[2:3]) / count
    var = (sums[3:4] + sums[4:5] + sums[5:6]) / count - mean * mean
    scale = lax.rsqrt(var + 1e-05)
    return scale, -mean * scale


def silu(u):
    half = 0.5 * u
    return half + half * jnp.tanh(half)


def conv_input(act_ref, main, tail, group_map):
    scale, shift = group_scale(main, tail, group_map)
    column = lax.broadcasted_iota(jnp.int32, (CELLS, 1), 0) % COLS

    def three(value, lo, hi):
        act = silu(value * scale[:, lo:hi] + shift[:, lo:hi])
        before = jnp.where(column == 0, 0.0, pltpu.roll(act, 1, 0))
        after = jnp.where(column == COLS - 1, 0.0, pltpu.roll(act, CELLS - 1, 0))
        return before, act, after

    for index, value in enumerate(three(main, 0, MAIN)):
        act_ref[:, index * MAIN : (index + 1) * MAIN] = value.astype(BF16)
    before, act, after = three(tail, MAIN, C)
    base = 3 * MAIN
    act_ref[:, base : base + 2 * TAIL] = jnp.concatenate([before, act], axis=1).astype(BF16)
    zero = jnp.zeros_like(after)
    act_ref[:, base + 2 * TAIL :] = jnp.concatenate([after, zero], axis=1).astype(BF16)


def conv_rows(act_ref, weight_ref, taps_ref):
    taps_ref[...] = dot32(act_ref[...], weight_ref[...])

    def joined(base, width):
        rows = []
        for row in range(4):
            total = None
            for dy in range(3):
                source = row + dy - 1
                if 0 <= source < 4:
                    piece = taps_ref[
                        source * COLS : (source + 1) * COLS,
                        base + dy * width : base + (dy + 1) * width,
                    ]
                    total = piece if total is None else total + piece
            rows.append(total)
        return jnp.concatenate(rows, axis=0)

    return joined(0, MAIN), joined(3 * MAIN, TAIL)


def block_kernel(
    own_ref, got_ref, first_ref, second_ref, emb_ref, group_ref, out_ref,
    x_ref, act_ref, taps_ref, res_ref, w1_ref, w2_ref, sems,
):
    here = lax.axis_index("height")
    copies = []
    for frame in range(2):
        for side, source in ((here, own_ref.at[2 * here + frame]), (1 - here, got_ref.at[frame])):
            copies.append(
                pltpu.make_async_copy(
                    source, x_ref.at[frame, pl.ds(2 * side, 2)], sems.at[len(copies)]
                )
            )
    weights = [
        pltpu.make_async_copy(first_ref, w1_ref, sems.at[4]),
        pltpu.make_async_copy(second_ref, w2_ref, sems.at[5]),
    ]
    for copy in copies + weights:
        copy.start()
    group_map = group_ref[...]

    def hidden(frame):
        value = x_ref[frame].reshape(CELLS, C).astype(F32)
        return value[:, :MAIN], value[:, MAIN:]

    for frame in range(2):
        copies[2 * frame].wait()
        copies[2 * frame + 1].wait()
        conv_input(act_ref.at[frame], *hidden(frame), group_map)
    weights[0].wait()
    for frame in range(2):
        main, tail = conv_rows(act_ref.at[frame], w1_ref, taps_ref.at[frame])
        emb = emb_ref[pl.ds(2 * here + frame, 1), :]
        conv_input(
            act_ref.at[frame], main + emb[:, :MAIN], tail + emb[:, MAIN:], group_map
        )
    weights[1].wait()
    for frame in range(2):
        main, tail = conv_rows(act_ref.at[frame], w2_ref, taps_ref.at[frame])
        old_main, old_tail = hidden(frame)
        res_ref[frame, :, :MAIN] = main + old_main
        res_ref[frame, :, MAIN:] = tail + old_tail
    for t in range(4):
        for h in range(2):
            for b in range(8):
                start = 256 * h + 64 * t + 8 * b
                pair = [res_ref[f, start : start + 8, :] for f in range(2)]
                out_ref[2 * t + h, b] = jnp.concatenate(pair, axis=0).astype(BF16)


def attention_kernel(
    base_ref, own_ref, prev_ref, next_ref, gain_ref, wq_ref, wkv_ref, wo_ref, out_ref,
    norm_ref, q_ref, kv_ref, att_ref,
):
    base = base_ref[0, 0]
    gain = gain_ref[...]
    for b in range(8):
        value = jnp.concatenate(
            [
                prev_ref[:, b].reshape(64, C),
                own_ref[:, b].reshape(128, C),
                next_ref[:, b].reshape(64, C),
            ],
            axis=0,
        ).astype(F32)
        mean = jnp.mean(value, axis=-1, keepdims=True)
        centred = value - mean
        var = jnp.mean(centred * centred, axis=-1, keepdims=True)
        normed = (centred * lax.rsqrt(var + 1e-05) * gain).astype(BF16)
        norm_ref[b] = normed
    for b in range(8):
        normed = norm_ref[b]
        q_ref[b] = dot32(normed[64:192], wq_ref[...]).astype(BF16)
        kv_ref[b] = dot32(normed, wkv_ref[...]).astype(BF16)
    row = lax.broadcasted_iota(jnp.int32, (128, 256), 0)
    col = lax.broadcasted_iota(jnp.int32, (128, 256), 1)
    away = col // 8 - 8 - row // 8
    frame = base + col // 8 - 8
    keep = (row % 8 == col % 8) & (away >= -(WINDOW // 2)) & (away < WINDOW // 2)
    keep = keep & (frame >= 0) & (frame < 256)
    bias = jnp.where(keep, 0.0, -1e30).astype(F32)
    bias2 = jnp.concatenate([bias, bias], axis=0)
    ones = jnp.ones((256, 128), BF16)
    lane = lax.broadcasted_iota(jnp.int32, (128, 128), 1)
    for b in range(8):
        for pair in range(3):
            low = 128 * pair
            q = q_ref[b, :, low : low + 128]
            k = kv_ref[b, :, low : low + 128]
            v = kv_ref[b, :, 384 + low : 384 + low + 128]
            zero = jnp.zeros_like(q)
            q0 = jnp.where(lane < 64, q, zero)
            if pair < 2:
                q = jnp.concatenate([q0, jnp.where(lane < 64, zero, q)], axis=0)
                add = bias2
            else:
                q = q0
                add = bias
            score = lax.dot_general(
                q, k, (((1,), (1,)), ((), ())), preferred_element_type=F32
            )
            probs = jnp.exp(score + add).astype(BF16)
            mixed = dot32(probs, jnp.concatenate([v, ones], axis=1))
            mixed = mixed[:, :128] / mixed[:, 128:]
            if pair < 2:
                mixed = jnp.where(lane < 64, mixed[:128], mixed[128:])
            att_ref[b, :, low : low + 128] = mixed.astype(BF16)
    for two in range(4):
        parts = []
        for b in (2 * two, 2 * two + 1):
            value = dot32(att_ref[b][:, :C], wo_ref[...])
            parts.append(value + own_ref[:, b].reshape(128, C).astype(F32))
        for f in range(16):
            rows = jnp.concatenate([p[8 * f : 8 * f + 8] for p in parts], axis=0)
            out_ref[f // 4, f % 4, 16 * two : 16 * two + 16, :] = rows.astype(BF16)


def vmem(count):
    return [pl.BlockSpec(memory_space=pltpu.VMEM)] * count


def body(
    latents, levels, conv_first, emb_weight, conv_second, ln_gain, w_query, w_key, w_value, w_out
):
    here = lax.axis_index("height")
    tm = lax.axis_index("tm")
    send = lax.dynamic_slice_in_dim(latents, 2 * (1 - here), 2, axis=0)
    got = lax.ppermute(send, "height", [(0, 1), (1, 0)])
    first, second = pack_conv(conv_first), pack_conv(conv_second)
    emb = level_embedding(levels, emb_weight)
    ids = jnp.arange(C) // (C // GROUPS)
    group_map = (ids[:, None] == ids[None, :]).astype(BF16)
    wide = ((0, 0), (0, 64))
    wq = jnp.pad(w_query * jnp.asarray(0.125, BF16), wide)
    wkv = jnp.concatenate([jnp.pad(w_key, wide), jnp.pad(w_value, wide)], axis=1)

    chunks = pl.pallas_call(
        block_kernel,
        out_shape=jax.ShapeDtypeStruct((8, 8, 16, C), BF16),
        in_specs=[pl.BlockSpec(memory_space=pl.ANY)] * 4 + vmem(2),
        out_specs=pl.BlockSpec(memory_space=pltpu.VMEM),
        scratch_shapes=[
            pltpu.VMEM((2, 4, COLS, C), BF16),
            pltpu.VMEM((2, CELLS, 1024), BF16),
            pltpu.VMEM((2, CELLS, 960), F32),
            pltpu.VMEM((2, CELLS, C), F32),
            pltpu.VMEM((1024, 960), BF16),
            pltpu.VMEM((1024, 960), BF16),
            pltpu.SemaphoreType.DMA((6,)),
        ],
        compiler_params=pltpu.CompilerParams(vmem_limit_bytes=40 * 2**20),
        name="resblock",
    )(latents, got, first, second, emb, group_map)

    size = lax.axis_size("tm")
    rings = [[8 * i + j for j in range(8)] for i in range(size // 4)]
    own = lax.all_to_all(chunks, AXES, 0, 0, tiled=True, axis_index_groups=rings)
    up = [(i, i + 4) for i in range(size - 4)]
    prev = lax.ppermute(own[4:], "tm", up)
    later = lax.ppermute(own[:4], "tm", [(j, i) for i, j in up])
    base = (tm // 4 * 16).astype(jnp.int32).reshape(1, 1)
    mixed = pl.pallas_call(
        attention_kernel,
        out_shape=jax.ShapeDtypeStruct((4, 4, 64, C), BF16),
        in_specs=[pl.BlockSpec(memory_space=pltpu.SMEM)] + vmem(7),
        out_specs=pl.BlockSpec(memory_space=pltpu.VMEM),
        scratch_shapes=[
            pltpu.VMEM((8, 256, C), BF16),
            pltpu.VMEM((8, 128, 384), BF16),
            pltpu.VMEM((8, 256, 768), BF16),
            pltpu.VMEM((8, 128, 384), BF16),
        ],
        compiler_params=pltpu.CompilerParams(vmem_limit_bytes=40 * 2**20),
        name="window_attention",
    )(base, own, prev, later, ln_gain.reshape(1, C), wq, wkv, w_out)
    quads = [[4 * i + j for j in range(4)] for i in range(size // 4)]
    home = lax.all_to_all(mixed, "tm", 0, 0, tiled=True, axis_index_groups=quads)
    return jnp.transpose(home, (1, 0, 2, 3)).reshape(4, 2, COLS, C)


def solution(mesh):
    placed = (P("tm", "height", None, None), P("tm"), P(), P(), P(), P(), P(), P(), P(), P())
    return jax.shard_map(
        body, mesh=mesh, in_specs=placed, out_specs=P("tm", "height", None, None), check_vma=False
    )
```

```python
import functools
import math

import jax
import jax.numpy as jnp
from jax import lax
from jax.experimental import pallas as pl
from jax.experimental.pallas import tpu as pltpu
from jax.sharding import PartitionSpec as P

HEADS = 5
GROUPS = 32
WINDOW = 16
C = 320
MAIN = 256
TAIL = C - MAIN
COLS = 128
CELLS = 512
AXES = ("tm", "height")
F32 = jnp.float32
BF16 = jnp.bfloat16


def dot32(a, b):
    return jnp.dot(a, b, preferred_element_type=F32)


def pack_kernel(first_ref, second_ref, first_out, second_out):
    for source, target in ((first_ref, first_out), (second_ref, second_out)):
        for dx in range(3):
            for lo, hi, row in ((0, MAIN, dx * MAIN), (MAIN, C, 3 * MAIN + dx * TAIL)):
                rows = slice(row, row + hi - lo)
                for dy in range(3):
                    target[rows, dy * MAIN : (dy + 1) * MAIN] = source[dy, dx, lo:hi, :MAIN]
                tails = [source[dy, dx, lo:hi, MAIN:] for dy in range(3)]
                target[rows, 3 * MAIN :] = jnp.concatenate(tails, axis=1)
        target[3 * C :, :] = jnp.zeros((TAIL, 3 * C), BF16)


def level_embedding(levels, emb_weight):
    half = emb_weight.shape[0] // 2
    freqs = jnp.exp(-math.log(10000.0) * jnp.arange(half).astype(jnp.float32) / half)
    angles = levels.astype(jnp.float32)[:, None] * freqs[None, :]
    sinus = jnp.concatenate([jnp.cos(angles), jnp.sin(angles)], axis=1)
    return jnp.dot(
        jax.nn.silu(sinus).astype(jnp.bfloat16), emb_weight, preferred_element_type=jnp.float32
    )


def split3(row):
    first = row.astype(BF16)
    rest = row - first.astype(F32)
    second = rest.astype(BF16)
    return [first, second, (rest - second.astype(F32)).astype(BF16)]


def group_scale(main, tail, group_map):
    parts = []
    for value in (main, tail):
        total = jnp.sum(value, axis=0, keepdims=True)
        square = jnp.sum(value * value, axis=0, keepdims=True)
        rows = split3(total) + split3(square)
        rows = [r.astype(F32) for r in rows] + [jnp.zeros_like(total)] * 2
        parts.append(jnp.concatenate(rows, axis=0).astype(BF16))
    sums = dot32(parts[0], group_map[:MAIN, :]) + dot32(parts[1], group_map[MAIN:, :])
    count = CELLS * (C // GROUPS)
    mean = (sums[0:1] + sums[1:2] + sums[2:3]) / count
    var = (sums[3:4] + sums[4:5] + sums[5:6]) / count - mean * mean
    scale = lax.rsqrt(var + 1e-05)
    return scale, -mean * scale


def silu(u):
    half = 0.5 * u
    return half + half * jnp.tanh(half)


def conv_input(act_ref, main, tail, group_map):
    scale, shift = group_scale(main, tail, group_map)
    column = lax.broadcasted_iota(jnp.int32, (CELLS, 1), 0) % COLS

    def three(value, lo, hi):
        act = silu(value * scale[:, lo:hi] + shift[:, lo:hi])
        before = jnp.where(column == 0, 0.0, pltpu.roll(act, 1, 0))
        after = jnp.where(column == COLS - 1, 0.0, pltpu.roll(act, CELLS - 1, 0))
        return before, act, after

    for index, value in enumerate(three(main, 0, MAIN)):
        act_ref[:, index * MAIN : (index + 1) * MAIN] = value.astype(BF16)
    before, act, after = three(tail, MAIN, C)
    base = 3 * MAIN
    act_ref[:, base : base + 2 * TAIL] = jnp.concatenate([before, act], axis=1).astype(BF16)
    zero = jnp.zeros_like(after)
    act_ref[:, base + 2 * TAIL :] = jnp.concatenate([after, zero], axis=1).astype(BF16)


def conv_rows(act_ref, weight_ref, taps_ref):
    taps_ref[...] = dot32(act_ref[...], weight_ref[...])

    def joined(base, width):
        rows = []
        for row in range(4):
            total = None
            for dy in range(3):
                source = row + dy - 1
                if 0 <= source < 4:
                    piece = taps_ref[
                        source * COLS : (source + 1) * COLS,
                        base + dy * width : base + (dy + 1) * width,
                    ]
                    total = piece if total is None else total + piece
            rows.append(total)
        return jnp.concatenate(rows, axis=0)

    return joined(0, MAIN), joined(3 * MAIN, TAIL)


def block_kernel(
    own_ref, got_ref, first_ref, second_ref, emb_ref, group_ref, *rest
):
    outs, (raw_ref, x_ref, act_ref, taps_ref, res_ref, w1_ref, w2_ref, sems) = rest[:8], rest[8:]
    here = lax.axis_index("height")
    ring = 2 * lax.rem(lax.axis_index("tm"), 4) + here
    copies = []
    for frame in range(2):
        for side, source in ((here, own_ref.at[2 * here + frame]), (1 - here, got_ref.at[frame])):
            copies.append(
                pltpu.make_async_copy(
                    source, raw_ref.at[frame, pl.ds(2 * side, 2)], sems.at[len(copies)]
                )
            )
    weights = [
        pltpu.make_async_copy(first_ref, w1_ref, sems.at[4]),
        pltpu.make_async_copy(second_ref, w2_ref, sems.at[5]),
    ]
    for copy in copies + weights:
        copy.start()
    group_map = group_ref[...]

    def hidden(frame):
        return x_ref[frame, :, :MAIN], x_ref[frame, :, MAIN:]

    for frame in range(2):
        copies[2 * frame].wait()
        copies[2 * frame + 1].wait()
        for row in range(4):
            x_ref[frame, row * COLS : (row + 1) * COLS, :] = raw_ref[frame, row].astype(F32).T
        conv_input(act_ref.at[frame], *hidden(frame), group_map)
    weights[0].wait()
    for frame in range(2):
        main, tail = conv_rows(act_ref.at[frame], w1_ref, taps_ref.at[frame])
        emb = emb_ref[pl.ds(2 * here + frame, 1), :]
        conv_input(
            act_ref.at[frame], main + emb[:, :MAIN], tail + emb[:, MAIN:], group_map
        )
    weights[1].wait()
    for frame in range(2):
        main, tail = conv_rows(act_ref.at[frame], w2_ref, taps_ref.at[frame])
        old_main, old_tail = hidden(frame)
        res_ref[frame, :, :MAIN] = main + old_main
        res_ref[frame, :, MAIN:] = tail + old_tail
    for k in range(8):
        other = lax.bitwise_xor(ring, k)
        base = 256 * lax.rem(other, 2) + 64 * lax.div(other, 2)
        for b in range(8):
            start = pl.multiple_of(base + 8 * b, 8)
            pair = [res_ref[f, pl.ds(start, 8), :] for f in range(2)]
            outs[k][b] = jnp.concatenate(pair, axis=0).astype(BF16)


def gather_kernel(*refs):
    pieces, (own_ref, near_ref, far_ref) = refs[:8], refs[8:]
    tm = lax.axis_index("tm")
    ring = 2 * lax.rem(tm, 4) + lax.axis_index("height")
    odd = lax.rem(lax.div(tm, 4), 2)
    for k in range(8):
        own_ref[lax.bitwise_xor(ring, k)] = pieces[k][...]
    for j in range(4):
        near_ref[j] = own_ref[4 * (1 - odd) + j]
        far_ref[j] = own_ref[4 * odd + j]


def attention_kernel(
    own_ref, near_ref, far_ref, gain_ref, wq_ref, wk_ref, wv_ref, wo_ref, *rest
):
    outs, (halo_ref, norm_ref, q_ref, kv_ref, att_ref, mixed_ref) = rest[:4], rest[4:]
    tm = lax.axis_index("tm")
    quad = lax.rem(tm, 4)
    base = lax.div(tm, 4) * 16
    odd = lax.rem(lax.div(tm, 4), 2)
    halo_ref[1 - odd] = near_ref[...]
    halo_ref[odd] = far_ref[...]
    gain = gain_ref[...]
    for b in range(8):
        value = jnp.concatenate(
            [
                halo_ref[0, :, b].reshape(64, C),
                own_ref[:, b].reshape(128, C),
                halo_ref[1, :, b].reshape(64, C),
            ],
            axis=0,
        ).astype(F32)
        mean = jnp.mean(value, axis=-1, keepdims=True)
        centred = value - mean
        var = jnp.mean(centred * centred, axis=-1, keepdims=True)
        normed = (centred * lax.rsqrt(var + 1e-05) * gain).astype(BF16)
        norm_ref[b] = normed
    pad = jnp.zeros((256, TAIL), BF16)
    for b in range(8):
        normed = norm_ref[b]
        q_ref[b, :, :C] = (dot32(normed[64:192], wq_ref[...]) * 0.125).astype(BF16)
        q_ref[b, :, C:] = pad[:128]
        for at, ref in ((0, wk_ref), (384, wv_ref)):
            kv_ref[b, :, at : at + C] = dot32(normed, ref[...]).astype(BF16)
            kv_ref[b, :, at + C : at + 384] = pad
    row = lax.broadcasted_iota(jnp.int32, (128, 256), 0)
    col = lax.broadcasted_iota(jnp.int32, (128, 256), 1)
    away = col // 8 - 8 - row // 8
    frame = base + col // 8 - 8
    keep = (row % 8 == col % 8) & (away >= -(WINDOW // 2)) & (away < WINDOW // 2)
    keep = keep & (frame >= 0) & (frame < 4 * lax.axis_size("tm"))
    bias = jnp.where(keep, 0.0, -1e30).astype(F32)
    bias2 = jnp.concatenate([bias, bias], axis=0)
    ones = jnp.ones((256, 128), BF16)
    lane = lax.broadcasted_iota(jnp.int32, (128, 128), 1)
    for b in range(8):
        for pair in range(3):
            low = 128 * pair
            q = q_ref[b, :, low : low + 128]
            k = kv_ref[b, :, low : low + 128]
            v = kv_ref[b, :, 384 + low : 384 + low + 128]
            add = bias
            if pair < 2:
                zero = jnp.zeros_like(q)
                q = jnp.concatenate(
                    [jnp.where(lane < 64, q, zero), jnp.where(lane < 64, zero, q)], axis=0
                )
                add = bias2
            score = lax.dot_general(
                q, k, (((1,), (1,)), ((), ())), preferred_element_type=F32
            )
            probs = jnp.exp(score + add).astype(BF16)
            mixed = dot32(probs, jnp.concatenate([v, ones], axis=1))
            mixed = mixed[:, :128] / mixed[:, 128:]
            if pair < 2:
                mixed = jnp.where(lane < 64, mixed[:128], mixed[128:])
            att_ref[b, :, low : low + 128] = mixed.astype(BF16)
    for two in range(4):
        parts = []
        for b in (2 * two, 2 * two + 1):
            value = dot32(att_ref[b][:, :C], wo_ref[...])
            parts.append(value + own_ref[:, b].reshape(128, C).astype(F32))
        for f in range(16):
            rows = jnp.concatenate([p[8 * f : 8 * f + 8] for p in parts], axis=0)
            mixed_ref[f, 16 * two : 16 * two + 16, :] = rows.astype(BF16)
    for k in range(4):
        other = lax.bitwise_xor(quad, k)
        for f in range(4):
            outs[k][f] = mixed_ref[4 * other + f]


def home_kernel(*refs):
    pieces, out_ref, cells_ref = refs[:4], refs[4], refs[5]
    quad = lax.rem(lax.axis_index("tm"), 4)
    for k in range(4):
        start = pl.multiple_of(64 * lax.bitwise_xor(quad, k), 64)
        for f in range(4):
            cells_ref[f, pl.ds(start, 64), :] = pieces[k][f]
    for f in range(4):
        for row in range(2):
            value = cells_ref[f, row * COLS : (row + 1) * COLS, :].astype(F32)
            out_ref[f, row] = value.T.astype(BF16)


def vmem(count):
    return [pl.BlockSpec(memory_space=pltpu.VMEM)] * count


def body(
    latents, levels, conv_first, emb_weight, conv_second, ln_gain, w_query, w_key, w_value, w_out
):
    here = lax.axis_index("height")
    size = lax.axis_size("tm")
    latents = jnp.transpose(latents, (0, 1, 3, 2))
    send = lax.dynamic_slice_in_dim(latents, 2 * (1 - here), 2, axis=0)
    got = lax.ppermute(send, "height", [(0, 1), (1, 0)])
    first, second = pl.pallas_call(
        pack_kernel,
        out_shape=[jax.ShapeDtypeStruct((1024, 3 * C), BF16)] * 2,
        in_specs=vmem(2),
        out_specs=vmem(2),
        compiler_params=pltpu.CompilerParams(vmem_limit_bytes=40 * 2**20),
        cost_estimate=pl.CostEstimate(flops=0, bytes_accessed=8_000_000, transcendentals=0),
        name="pack_weights",
    )(conv_first, conv_second)
    emb = level_embedding(levels, emb_weight)
    ids = jnp.arange(C) // (C // GROUPS)
    group_map = (ids[:, None] == ids[None, :]).astype(BF16)

    pieces = pl.pallas_call(
        block_kernel,
        out_shape=[jax.ShapeDtypeStruct((8, 16, C), BF16)] * 8,
        in_specs=[pl.BlockSpec(memory_space=pl.ANY)] * 4 + vmem(2),
        out_specs=vmem(8),
        scratch_shapes=[
            pltpu.VMEM((2, 4, C, COLS), BF16),
            pltpu.VMEM((2, CELLS, C), F32),
            pltpu.VMEM((2, CELLS, 1024), BF16),
            pltpu.VMEM((2, CELLS, 960), F32),
            pltpu.VMEM((2, CELLS, C), F32),
            pltpu.VMEM((1024, 960), BF16),
            pltpu.VMEM((1024, 960), BF16),
            pltpu.SemaphoreType.DMA((6,)),
        ],
        compiler_params=pltpu.CompilerParams(vmem_limit_bytes=40 * 2**20),
        name="resblock",
    )(latents, got, first, second, emb, group_map)

    swaps = [[(i, i ^ k) for i in range(2 * size)] for k in range(8)]
    pieces = [pieces[0]] + [lax.ppermute(pieces[k], AXES, swaps[k]) for k in range(1, 8)]
    half = jax.ShapeDtypeStruct((4, 8, 16, C), BF16)
    own, near, far = pl.pallas_call(
        gather_kernel,
        out_shape=[jax.ShapeDtypeStruct((8, 8, 16, C), BF16), half, half],
        in_specs=vmem(8),
        out_specs=vmem(3),
        compiler_params=pltpu.CompilerParams(vmem_limit_bytes=40 * 2**20),
        name="by_frame",
    )(*pieces)
    up = [(i, i + 4) for i in range(size - 4) if i // 4 % 2 == 1]
    far = lax.ppermute(far, "tm", up + [(j, i) for i, j in up])
    near = lax.ppermute(near, "tm", [(i, i ^ 4) for i in range(size)])
    pieces = pl.pallas_call(
        attention_kernel,
        out_shape=[jax.ShapeDtypeStruct((4, 64, C), BF16)] * 4,
        in_specs=vmem(8),
        out_specs=vmem(4),
        scratch_shapes=[
            pltpu.VMEM((2, 4, 8, 16, C), BF16),
            pltpu.VMEM((8, 256, C), BF16),
            pltpu.VMEM((8, 128, 384), BF16),
            pltpu.VMEM((8, 256, 768), BF16),
            pltpu.VMEM((8, 128, 384), BF16),
            pltpu.VMEM((16, 64, C), BF16),
        ],
        compiler_params=pltpu.CompilerParams(vmem_limit_bytes=40 * 2**20),
        name="window_attention",
    )(own, near, far, ln_gain.reshape(1, C), w_query, w_key, w_value, w_out)
    swaps = [[(i, i ^ k) for i in range(size)] for k in range(4)]
    pieces = [pieces[0]] + [lax.ppermute(pieces[k], "tm", swaps[k]) for k in range(1, 4)]
    home = pl.pallas_call(
        home_kernel,
        out_shape=jax.ShapeDtypeStruct((4, 2, C, COLS), BF16),
        in_specs=vmem(4),
        out_specs=pl.BlockSpec(memory_space=pltpu.VMEM),
        scratch_shapes=[pltpu.VMEM((4, 256, C), BF16)],
        compiler_params=pltpu.CompilerParams(vmem_limit_bytes=40 * 2**20),
        name="home",
    )(*pieces)
    return jnp.transpose(home, (0, 1, 3, 2))


def solution(mesh):
    placed = (P("tm", "height", None, None), P("tm"), P(), P(), P(), P(), P(), P(), P(), P())
    return jax.shard_map(
        body, mesh=mesh, in_specs=placed, out_specs=P("tm", "height", None, None), check_vma=False
    )
```

```python
import functools
import math

import jax
import jax.numpy as jnp
from jax import lax
from jax.experimental import pallas as pl
from jax.experimental.pallas import tpu as pltpu
from jax.sharding import PartitionSpec as P

HEADS = 5
GROUPS = 32
WINDOW = 16
C = 320
MAIN = 256
TAIL = C - MAIN
COLS = 128
CELLS = 512
AXES = ("tm", "height")
F32 = jnp.float32
BF16 = jnp.bfloat16


def dot32(a, b):
    return jnp.dot(a, b, preferred_element_type=F32)


def pack_kernel(first_ref, second_ref, first_out, second_out):
    for source, target in ((first_ref, first_out), (second_ref, second_out)):
        for dx in range(3):
            for lo, hi, row in ((0, MAIN, dx * MAIN), (MAIN, C, 3 * MAIN + dx * TAIL)):
                rows = slice(row, row + hi - lo)
                for dy in range(3):
                    target[rows, dy * MAIN : (dy + 1) * MAIN] = source[dy, dx, lo:hi, :MAIN]
                tails = [source[dy, dx, lo:hi, MAIN:] for dy in range(3)]
                target[rows, 3 * MAIN :] = jnp.concatenate(tails, axis=1)
        target[3 * C :, :] = jnp.zeros((TAIL, 3 * C), BF16)


def level_embedding(levels, emb_weight):
    half = emb_weight.shape[0] // 2
    freqs = jnp.exp(-math.log(10000.0) * jnp.arange(half).astype(jnp.float32) / half)
    angles = levels.astype(jnp.float32)[:, None] * freqs[None, :]
    sinus = jnp.concatenate([jnp.cos(angles), jnp.sin(angles)], axis=1)
    return jnp.dot(
        jax.nn.silu(sinus).astype(jnp.bfloat16), emb_weight, preferred_element_type=jnp.float32
    )


def split3(row):
    first = row.astype(BF16)
    rest = row - first.astype(F32)
    second = rest.astype(BF16)
    return [first, second, (rest - second.astype(F32)).astype(BF16)]


def group_scale(main, tail, group_map):
    parts = []
    for value in (main, tail):
        total = jnp.sum(value, axis=0, keepdims=True)
        square = jnp.sum(value * value, axis=0, keepdims=True)
        rows = split3(total) + split3(square)
        rows = [r.astype(F32) for r in rows] + [jnp.zeros_like(total)] * 2
        parts.append(jnp.concatenate(rows, axis=0).astype(BF16))
    sums = dot32(parts[0], group_map[:MAIN, :]) + dot32(parts[1], group_map[MAIN:, :])
    count = CELLS * (C // GROUPS)
    mean = (sums[0:1] + sums[1:2] + sums[2:3]) / count
    var = (sums[3:4] + sums[4:5] + sums[5:6]) / count - mean * mean
    scale = lax.rsqrt(var + 1e-05)
    return scale, -mean * scale


def silu(u):
    half = 0.5 * u
    return half + half * jnp.tanh(half)


def conv_input(act_ref, main, tail, group_map):
    scale, shift = group_scale(main, tail, group_map)
    column = lax.broadcasted_iota(jnp.int32, (CELLS, 1), 0) % COLS

    def three(value, lo, hi):
        act = silu(value * scale[:, lo:hi] + shift[:, lo:hi])
        before = jnp.where(column == 0, 0.0, pltpu.roll(act, 1, 0))
        after = jnp.where(column == COLS - 1, 0.0, pltpu.roll(act, CELLS - 1, 0))
        return before, act, after

    for index, value in enumerate(three(main, 0, MAIN)):
        act_ref[:, index * MAIN : (index + 1) * MAIN] = value.astype(BF16)
    before, act, after = three(tail, MAIN, C)
    base = 3 * MAIN
    act_ref[:, base : base + 2 * TAIL] = jnp.concatenate([before, act], axis=1).astype(BF16)
    zero = jnp.zeros_like(after)
    act_ref[:, base + 2 * TAIL :] = jnp.concatenate([after, zero], axis=1).astype(BF16)


def conv_rows(act_ref, weight_ref, taps_ref):
    taps_ref[...] = dot32(act_ref[...], weight_ref[...])

    def joined(base, width):
        rows = []
        for row in range(4):
            total = None
            for dy in range(3):
                source = row + dy - 1
                if 0 <= source < 4:
                    piece = taps_ref[
                        source * COLS : (source + 1) * COLS,
                        base + dy * width : base + (dy + 1) * width,
                    ]
                    total = piece if total is None else total + piece
            rows.append(total)
        return jnp.concatenate(rows, axis=0)

    return joined(0, MAIN), joined(3 * MAIN, TAIL)


def block_kernel(
    frame, own_ref, got_ref, first_ref, second_ref, emb_ref, group_ref, *rest
):
    x_ref, act_ref, taps_ref, res_ref = rest[-4:]
    here = lax.axis_index("height")
    ring = 2 * lax.rem(lax.axis_index("tm"), 4) + here
    group_map = group_ref[...]
    for row in range(2):
        for side, raw in ((here, own_ref[2 * here + frame, row]), (1 - here, got_ref[0, row])):
            start = pl.multiple_of((2 * side + row) * COLS, COLS)
            x_ref[pl.ds(start, COLS), :] = raw.astype(F32).T

    def hidden():
        return x_ref[:, :MAIN], x_ref[:, MAIN:]

    conv_input(act_ref, *hidden(), group_map)
    main, tail = conv_rows(act_ref, first_ref, taps_ref)
    emb = emb_ref[pl.ds(2 * here + frame, 1), :]
    conv_input(act_ref, main + emb[:, :MAIN], tail + emb[:, MAIN:], group_map)
    main, tail = conv_rows(act_ref, second_ref, taps_ref)
    old_main, old_tail = hidden()
    target = rest[0] if frame == 0 else res_ref
    target[:, :MAIN] = main + old_main
    target[:, MAIN:] = tail + old_tail
    if frame == 0:
        return
    before_ref, outs = rest[0], rest[1:9]
    for k in range(8):
        other = lax.bitwise_xor(ring, k)
        base = 256 * lax.rem(other, 2) + 64 * lax.div(other, 2)
        for b in range(8):
            rows = pl.ds(pl.multiple_of(base + 8 * b, 8), 8)
            pair = [before_ref[rows, :], res_ref[rows, :]]
            outs[k][b] = jnp.concatenate(pair, axis=0).astype(BF16)


def gather_kernel(*refs):
    pieces, (own_ref, near_refs, far_refs) = refs[:8], (refs[8], refs[9:11], refs[11:])
    tm = lax.axis_index("tm")
    ring = 2 * lax.rem(tm, 4) + lax.axis_index("height")
    odd = lax.rem(lax.div(tm, 4), 2)
    for k in range(8):
        own_ref[lax.bitwise_xor(ring, k)] = pieces[k][...]
    for part in range(2):
        for j in range(4):
            near_refs[part][j] = own_ref[4 * (1 - odd) + j, 4 * part : 4 * part + 4]
            far_refs[part][j] = own_ref[4 * odd + j, 4 * part : 4 * part + 4]


def project(value, gain, wk_ref, wv_ref, kv_ref, at):
    value = value.astype(F32)
    mean = jnp.mean(value, axis=-1, keepdims=True)
    centred = value - mean
    var = jnp.mean(centred * centred, axis=-1, keepdims=True)
    normed = (centred * lax.rsqrt(var + 1e-05) * gain).astype(BF16)
    rows = slice(at[1], at[1] + value.shape[0])
    pad = jnp.zeros((value.shape[0], TAIL), BF16)
    for low, ref in ((0, wk_ref), (384, wv_ref)):
        kv_ref[at[0], rows, low : low + C] = dot32(normed, ref[...]).astype(BF16)
        kv_ref[at[0], rows, low + C : low + 384] = pad
    return normed


def own_kernel(own_ref, gain_ref, wq_ref, wk_ref, wv_ref, q_ref, kv_ref):
    gain = gain_ref[...]
    for b in range(8):
        value = own_ref[:, b].reshape(128, C)
        normed = project(value, gain, wk_ref, wv_ref, kv_ref, (b, 0))
        q_ref[b, :, :C] = (dot32(normed, wq_ref[...]) * 0.125).astype(BF16)
        q_ref[b, :, C:] = jnp.zeros((128, TAIL), BF16)


def attention_kernel(
    part, own_ref, q_ref, mine_ref, far_ref, near_ref, gain_ref, wk_ref, wv_ref, wo_ref, *rest
):
    outs, (halo_ref, kv_ref, att_ref, mixed_ref) = rest[:4], rest[4:]
    tm = lax.axis_index("tm")
    quad = lax.rem(tm, 4)
    base = lax.div(tm, 4) * 16
    odd = lax.rem(lax.div(tm, 4), 2)
    halo_ref[1 - odd] = near_ref[...]
    halo_ref[odd] = far_ref[...]
    gain = gain_ref[...]
    for b in range(4):
        value = halo_ref[:, :, b].reshape(128, C)
        project(value, gain, wk_ref, wv_ref, kv_ref, (b, 0))
    row = lax.broadcasted_iota(jnp.int32, (128, 256), 0)
    col = lax.broadcasted_iota(jnp.int32, (128, 256), 1)
    key = jnp.where(col < 64, col // 8 - 8, jnp.where(col < 128, col // 8 + 8, col // 8 - 16))
    away = key - row // 8
    keep = (row % 8 == col % 8) & (away >= -(WINDOW // 2)) & (away < WINDOW // 2)
    keep = keep & (base + key >= 0) & (base + key < 4 * lax.axis_size("tm"))
    bias = jnp.where(keep, 0.0, -1e30).astype(F32)
    bias2 = jnp.concatenate([bias, bias], axis=0)
    ones = jnp.ones((256, 128), BF16)
    lane = lax.broadcasted_iota(jnp.int32, (128, 128), 1)
    for b in range(4):
        for pair in range(3):
            low = 128 * pair
            full = 4 * part + b
            q = q_ref[full, :, low : low + 128]
            k = [r[i, :, low : low + 128] for r, i in ((kv_ref, b), (mine_ref, full))]
            v = [r[i, :, 384 + low : 512 + low] for r, i in ((kv_ref, b), (mine_ref, full))]
            k, v = jnp.concatenate(k, axis=0), jnp.concatenate(v, axis=0)
            add = bias
            if pair < 2:
                zero = jnp.zeros_like(q)
                q = jnp.concatenate(
                    [jnp.where(lane < 64, q, zero), jnp.where(lane < 64, zero, q)], axis=0
                )
                add = bias2
            score = lax.dot_general(
                q, k, (((1,), (1,)), ((), ())), preferred_element_type=F32
            )
            probs = jnp.exp(score + add).astype(BF16)
            mixed = dot32(probs, jnp.concatenate([v, ones], axis=1))
            mixed = mixed[:, :128] / mixed[:, 128:]
            if pair < 2:
                mixed = jnp.where(lane < 64, mixed[:128], mixed[128:])
            att_ref[b, :, low : low + 128] = mixed.astype(BF16)
    for two in range(2):
        parts = []
        for b in (2 * two, 2 * two + 1):
            value = dot32(att_ref[b][:, :C], wo_ref[...])
            parts.append(value + own_ref[:, 4 * part + b].reshape(128, C).astype(F32))
        for f in range(16):
            rows = jnp.concatenate([p[8 * f : 8 * f + 8] for p in parts], axis=0)
            mixed_ref[f, 16 * two : 16 * two + 16, :] = rows.astype(BF16)
    for k in range(4):
        other = lax.bitwise_xor(quad, k)
        for f in range(4):
            outs[k][f] = mixed_ref[4 * other + f]


def home_kernel(*refs):
    pieces, out_ref, cells_ref = refs[:8], refs[8], refs[9]
    quad = lax.rem(lax.axis_index("tm"), 4)
    for k in range(4):
        for part in range(2):
            start = pl.multiple_of(64 * lax.bitwise_xor(quad, k) + 32 * part, 32)
            for f in range(4):
                cells_ref[f, pl.ds(start, 32), :] = pieces[4 * part + k][f]
    for f in range(4):
        for row in range(2):
            value = cells_ref[f, row * COLS : (row + 1) * COLS, :].astype(F32)
            out_ref[f, row] = value.T.astype(BF16)


def cost(flops):
    return pl.CostEstimate(flops=flops, bytes_accessed=0, transcendentals=0)


def vmem(count):
    return [pl.BlockSpec(memory_space=pltpu.VMEM)] * count


def body(
    latents, levels, conv_first, emb_weight, conv_second, ln_gain, w_query, w_key, w_value, w_out
):
    here = lax.axis_index("height")
    size = lax.axis_size("tm")
    latents = jnp.transpose(latents, (0, 1, 3, 2))
    got = []
    for frame in range(2):
        send = lax.dynamic_slice_in_dim(latents, 2 * (1 - here) + frame, 1, axis=0)
        got.append(lax.ppermute(send, "height", [(0, 1), (1, 0)]))
    params = pltpu.CompilerParams(vmem_limit_bytes=28 * 2**20)
    first, second = pl.pallas_call(
        pack_kernel,
        out_shape=[jax.ShapeDtypeStruct((1024, 3 * C), BF16)] * 2,
        in_specs=vmem(2),
        out_specs=vmem(2),
        compiler_params=params,
        cost_estimate=cost(1_000_000_000),
        name="pack_weights",
    )(conv_first, conv_second)
    emb = level_embedding(levels, emb_weight)
    ids = jnp.arange(C) // (C // GROUPS)
    group_map = (ids[:, None] == ids[None, :]).astype(BF16)

    before = []
    for frame in range(2):
        piece = [jax.ShapeDtypeStruct((8, 16, C), BF16)] * 8
        whole = [jax.ShapeDtypeStruct((CELLS, C), F32)]
        pieces = pl.pallas_call(
            functools.partial(block_kernel, frame),
            out_shape=piece if frame else whole,
            in_specs=vmem(6 + frame),
            out_specs=vmem(8 if frame else 1),
            scratch_shapes=[
                pltpu.VMEM((CELLS, C), F32),
                pltpu.VMEM((CELLS, 1024), BF16),
                pltpu.VMEM((CELLS, 960), F32),
                pltpu.VMEM((CELLS, C), F32),
            ],
            compiler_params=params,
            cost_estimate=cost(4_000_000_000),
            name="resblock",
        )(latents, got[frame], first, second, emb, group_map, *before)
        before = pieces

    swaps = [[(i, i ^ k) for i in range(2 * size)] for k in range(8)]
    pieces = [pieces[0]] + [lax.ppermute(pieces[k], AXES, swaps[k]) for k in range(1, 8)]
    half = [jax.ShapeDtypeStruct((4, 4, 16, C), BF16)]
    own, *halves = pl.pallas_call(
        gather_kernel,
        out_shape=[jax.ShapeDtypeStruct((8, 8, 16, C), BF16)] + half * 4,
        in_specs=vmem(8),
        out_specs=vmem(5),
        compiler_params=params,
        name="by_frame",
    )(*pieces)
    up = [(i, i + 4) for i in range(size - 4) if i // 4 % 2 == 1]
    both = up + [(j, i) for i, j in up]
    far = [lax.ppermute(x, "tm", both) for x in halves[2:]]
    near = [lax.ppermute(x, "tm", [(i, i ^ 4) for i in range(size)]) for x in halves[:2]]
    gain = ln_gain.reshape(1, C)
    query, mine = pl.pallas_call(
        own_kernel,
        out_shape=[
            jax.ShapeDtypeStruct((8, 128, 384), BF16),
            jax.ShapeDtypeStruct((8, 128, 768), BF16),
        ],
        in_specs=vmem(5),
        out_specs=vmem(2),
        compiler_params=params,
        cost_estimate=cost(2_000_000_000),
        name="own_frames",
    )(own, gain, w_query, w_key, w_value)
    swaps = [[(i, i ^ k) for i in range(size)] for k in range(4)]
    back = []
    for part in range(2):
        pieces = pl.pallas_call(
            functools.partial(attention_kernel, part),
            out_shape=[jax.ShapeDtypeStruct((4, 32, C), BF16)] * 4,
            in_specs=vmem(9),
            out_specs=vmem(4),
            scratch_shapes=[
                pltpu.VMEM((2, 4, 4, 16, C), BF16),
                pltpu.VMEM((4, 128, 768), BF16),
                pltpu.VMEM((4, 128, 384), BF16),
                pltpu.VMEM((16, 32, C), BF16),
            ],
            compiler_params=params,
            cost_estimate=cost(2_000_000_000),
            name="window_attention",
        )(own, query, mine, far[part], near[part], gain, w_key, w_value, w_out)
        back += [pieces[0]] + [lax.ppermute(pieces[k], "tm", swaps[k]) for k in range(1, 4)]
    home = pl.pallas_call(
        home_kernel,
        out_shape=jax.ShapeDtypeStruct((4, 2, C, COLS), BF16),
        in_specs=vmem(8),
        out_specs=pl.BlockSpec(memory_space=pltpu.VMEM),
        scratch_shapes=[pltpu.VMEM((4, 256, C), BF16)],
        compiler_params=params,
        name="home",
    )(*back)
    return jnp.transpose(home, (0, 1, 3, 2))


def solution(mesh):
    placed = (P("tm", "height", None, None), P("tm"), P(), P(), P(), P(), P(), P(), P(), P())
    return jax.shard_map(
        body, mesh=mesh, in_specs=placed, out_specs=P("tm", "height", None, None), check_vma=False
    )
```

```python
import functools
import math

import jax
import jax.numpy as jnp
from jax import lax
from jax.experimental import pallas as pl
from jax.experimental.pallas import tpu as pltpu
from jax.sharding import PartitionSpec as P

HEADS = 5
GROUPS = 32
WINDOW = 16
C = 320
MAIN = 256
TAIL = C - MAIN
COLS = 128
CELLS = 512
AXES = ("tm", "height")
F32 = jnp.float32
BF16 = jnp.bfloat16


def dot32(a, b):
    return jnp.dot(a, b, preferred_element_type=F32)


def pick(latents_ref, out_ref, sem, frame):
    there = 1 - lax.axis_index("height")
    return pltpu.make_async_copy(latents_ref.at[pl.ds(2 * there + frame, 1)], out_ref, sem)


def pick_kernel(latents_ref, out_ref, sem):
    copy = pick(latents_ref, out_ref, sem, 0)
    copy.start()
    copy.wait()


def pack_kernel(
    first_ref, second_ref, latents_ref, first_out, second_out, send_out, raw_ref, sems, sem
):
    send = pick(latents_ref, send_out, sem, 1)
    send.start()
    copies = []
    for index, ref in enumerate((first_ref, second_ref)):
        for dy in range(3):
            copies.append(
                pltpu.make_async_copy(ref.at[dy], raw_ref.at[index, dy], sems.at[index, dy])
            )
            copies[-1].start()
    for index, target in enumerate((first_out, second_out)):
        for copy in copies[3 * index : 3 * index + 3]:
            copy.wait()
        source = raw_ref.at[index]
        for dx in range(3):
            for lo, hi, row in ((0, MAIN, dx * MAIN), (MAIN, C, 3 * MAIN + dx * TAIL)):
                rows = slice(row, row + hi - lo)
                for dy in range(3):
                    target[rows, dy * MAIN : (dy + 1) * MAIN] = source[dy, dx, lo:hi, :MAIN]
                tails = [source[dy, dx, lo:hi, MAIN:] for dy in range(3)]
                target[rows, 3 * MAIN :] = jnp.concatenate(tails, axis=1)
        target[3 * C :, :] = jnp.zeros((TAIL, 3 * C), BF16)
    send.wait()


def in_hbm(array):
    return pltpu.with_memory_space_constraint(array, pltpu.HBM)


def level_embedding(levels, emb_weight):
    half = emb_weight.shape[0] // 2
    freqs = jnp.exp(-math.log(10000.0) * jnp.arange(half).astype(jnp.float32) / half)
    angles = levels.astype(jnp.float32)[:, None] * freqs[None, :]
    sinus = jnp.concatenate([jnp.cos(angles), jnp.sin(angles)], axis=1)
    return jnp.dot(
        jax.nn.silu(sinus).astype(jnp.bfloat16), emb_weight, preferred_element_type=jnp.float32
    )


def split3(row):
    first = row.astype(BF16)
    rest = row - first.astype(F32)
    second = rest.astype(BF16)
    return [first, second, (rest - second.astype(F32)).astype(BF16)]


def group_scale(main, tail, group_map):
    total = [jnp.sum(v, axis=0, keepdims=True) for v in (main, tail)]
    square = [jnp.sum(v * v, axis=0, keepdims=True) for v in (main, tail)]
    rows = split3(jnp.concatenate(total, axis=1)) + split3(jnp.concatenate(square, axis=1))
    rows = [r.astype(F32) for r in rows] + [jnp.zeros((2, C), F32)]
    sums = dot32(jnp.concatenate(rows, axis=0).astype(BF16), group_map)
    count = CELLS * (C // GROUPS)
    mean = (sums[0:1] + sums[1:2] + sums[2:3]) / count
    var = (sums[3:4] + sums[4:5] + sums[5:6]) / count - mean * mean
    scale = lax.rsqrt(var + 1e-05)
    return scale, -mean * scale


def silu(u):
    half = 0.5 * u
    return half + half * jnp.tanh(half)


def conv_input(act_ref, main, tail, group_map):
    scale, shift = group_scale(main, tail, group_map)
    column = lax.broadcasted_iota(jnp.int32, (CELLS, 1), 0) % COLS

    def three(value, lo, hi):
        act = silu(value * scale[:, lo:hi] + shift[:, lo:hi])
        before = jnp.where(column == 0, 0.0, pltpu.roll(act, 1, 0))
        after = jnp.where(column == COLS - 1, 0.0, pltpu.roll(act, CELLS - 1, 0))
        return before, act, after

    for index, value in enumerate(three(main, 0, MAIN)):
        act_ref[:, index * MAIN : (index + 1) * MAIN] = value.astype(BF16)
    before, act, after = three(tail, MAIN, C)
    base = 3 * MAIN
    act_ref[:, base : base + 2 * TAIL] = jnp.concatenate([before, act], axis=1).astype(BF16)
    zero = jnp.zeros_like(after)
    act_ref[:, base + 2 * TAIL :] = jnp.concatenate([after, zero], axis=1).astype(BF16)


def conv_rows(act_ref, weight_ref, taps_ref):
    taps_ref[...] = dot32(act_ref[...], weight_ref[...])

    def joined(base, width):
        rows = []
        for row in range(4):
            total = None
            for dy in range(3):
                source = row + dy - 1
                if 0 <= source < 4:
                    piece = taps_ref[
                        source * COLS : (source + 1) * COLS,
                        base + dy * width : base + (dy + 1) * width,
                    ]
                    total = piece if total is None else total + piece
            rows.append(total)
        return jnp.concatenate(rows, axis=0)

    return joined(0, MAIN), joined(3 * MAIN, TAIL)


def block_kernel(
    frame, own_ref, got_ref, first_ref, second_ref, emb_ref, group_ref, *rest
):
    x_ref, act_ref, taps_ref, res_ref = rest[-4:]
    here = lax.axis_index("height")
    ring = 2 * lax.rem(lax.axis_index("tm"), 4) + here
    group_map = group_ref[...]
    for row in range(2):
        for side, raw in ((here, own_ref[2 * here + frame, row]), (1 - here, got_ref[0, row])):
            start = pl.multiple_of((2 * side + row) * COLS, COLS)
            x_ref[pl.ds(start, COLS), :] = raw.astype(F32).T

    def hidden():
        return x_ref[:, :MAIN], x_ref[:, MAIN:]

    conv_input(act_ref, *hidden(), group_map)
    main, tail = conv_rows(act_ref, first_ref, taps_ref)
    emb = emb_ref[pl.ds(2 * here + frame, 1), :]
    conv_input(act_ref, main + emb[:, :MAIN], tail + emb[:, MAIN:], group_map)
    main, tail = conv_rows(act_ref, second_ref, taps_ref)
    old_main, old_tail = hidden()
    target = rest[0] if frame == 0 else res_ref
    target[:, :MAIN] = main + old_main
    target[:, MAIN:] = tail + old_tail
    if frame == 0:
        return
    before_ref, outs = rest[0], rest[1:9]
    for k in range(8):
        other = lax.bitwise_xor(ring, k)
        base = 256 * lax.rem(other, 2) + 64 * lax.div(other, 2)
        for b in range(8):
            rows = pl.ds(pl.multiple_of(base + 8 * b, 8), 8)
            pair = [before_ref[rows, :], res_ref[rows, :]]
            outs[k][b] = jnp.concatenate(pair, axis=0).astype(BF16)


def odd_ring():
    return lax.rem(lax.div(lax.axis_index("tm"), 4), 2)


def gather_kernel(*refs):
    pieces, (own_ref, near_refs, far_refs) = refs[:8], (refs[8], refs[9:11], refs[11:])
    ring = 2 * lax.rem(lax.axis_index("tm"), 4) + lax.axis_index("height")
    odd = odd_ring()
    for k in range(8):
        own_ref[lax.bitwise_xor(ring, k)] = pieces[k][...]
    for part in range(2):
        for j in range(4):
            near_refs[part][j] = own_ref[4 * (1 - odd) + j, 4 * part : 4 * part + 4]
            far_refs[part][j] = own_ref[4 * odd + j, 4 * part : 4 * part + 4]


def layer_norm(value, gain):
    value = value.astype(F32)
    mean = jnp.mean(value, axis=-1, keepdims=True)
    centred = value - mean
    var = jnp.mean(centred * centred, axis=-1, keepdims=True)
    return (centred * lax.rsqrt(var + 1e-05) * gain).astype(BF16)


def keys_values(blocks, gain_ref, wk_ref, wv_ref, norm_ref, kv_ref):
    gain = gain_ref[...]
    rows = blocks[0].shape[0]
    for b, value in enumerate(blocks):
        norm_ref[b * rows : (b + 1) * rows, :] = layer_norm(value, gain)
    each = len(blocks) if rows * len(blocks) <= 512 else 512 // rows
    for b in range(0, len(blocks), each):
        normed = norm_ref[b * rows : (b + each) * rows, :]
        for low, ref in ((0, wk_ref), (384, wv_ref)):
            value = dot32(normed, ref[...]).astype(BF16).reshape(each, rows, C)
            kv_ref[b : b + each, :, low : low + C] = value
            pad = jnp.zeros((each, rows, TAIL), BF16)
            kv_ref[b : b + each, :, low + C : low + 384] = pad


def own_kernel(own_ref, gain_ref, wq_ref, wk_ref, wv_ref, q_ref, kv_ref, norm_ref):
    blocks = [own_ref[:, b].reshape(128, C) for b in range(8)]
    keys_values(blocks, gain_ref, wk_ref, wv_ref, norm_ref, kv_ref)
    for b in range(0, 8, 4):
        value = dot32(norm_ref[128 * b : 128 * b + 512, :], wq_ref[...]) * 0.125
        q_ref[b : b + 4, :, :C] = value.astype(BF16).reshape(4, 128, C)
        q_ref[b : b + 4, :, C:] = jnp.zeros((4, 128, TAIL), BF16)


def attention_kernel(
    part, own_ref, q_ref, mine_ref, far_ref, near_ref, gain_ref, wk_ref, wv_ref, wo_ref, *rest
):
    outs, (norm_ref, kv_ref, att_ref, mixed_ref) = rest[:4], rest[4:]
    tm = lax.axis_index("tm")
    quad = lax.rem(tm, 4)
    base = lax.div(tm, 4) * 16
    odd = odd_ring()
    blocks = [
        jnp.concatenate([r[:, b].reshape(64, C) for r in (near_ref, far_ref)], axis=0)
        for b in range(4)
    ]
    keys_values(blocks, gain_ref, wk_ref, wv_ref, norm_ref, kv_ref)
    row = lax.broadcasted_iota(jnp.int32, (128, 256), 0)
    col = lax.broadcasted_iota(jnp.int32, (128, 256), 1)
    near_at, far_at = 16 - 24 * odd, 24 * odd - 16
    key = col // 8 + jnp.where(col < 64, near_at, jnp.where(col < 128, far_at, -16))
    away = key - row // 8
    keep = (row % 8 == col % 8) & (away >= -(WINDOW // 2)) & (away < WINDOW // 2)
    keep = keep & (base + key >= 0) & (base + key < 4 * lax.axis_size("tm"))
    bias = jnp.where(keep, 0.0, -1e30).astype(F32)
    bias2 = jnp.concatenate([bias, bias], axis=0)
    ones = jnp.ones((256, 128), BF16)
    lane = lax.broadcasted_iota(jnp.int32, (128, 128), 1)

    def keys(b, low):
        full = 4 * part + b
        sides = [kv_ref[b], mine_ref[full]]
        return jnp.concatenate([x[:, low : low + 128] for x in sides], axis=0)

    for first in range(0, 4, 2):
        items = [(b, 128 * pair) for b in (first, first + 1) for pair in range(3)]
        probs = []
        for b, low in items:
            q = q_ref[4 * part + b, :, low : low + 128]
            add = bias
            if low < 256:
                zero = jnp.zeros_like(q)
                q = jnp.concatenate(
                    [jnp.where(lane < 64, q, zero), jnp.where(lane < 64, zero, q)], axis=0
                )
                add = bias2
            score = lax.dot_general(
                q, keys(b, low), (((1,), (1,)), ((), ())), preferred_element_type=F32
            )
            probs.append(jnp.exp(score + add).astype(BF16))
        for (b, low), prob in zip(items, probs):
            mixed = dot32(prob, jnp.concatenate([keys(b, 384 + low), ones], axis=1))
            mixed = mixed[:, :128] / mixed[:, 128:]
            if low < 256:
                mixed = jnp.where(lane < 64, mixed[:128], mixed[128:])
            att_ref[b, :, low : low + 128] = mixed.astype(BF16)
    for two in range(2):
        parts = []
        for b in (2 * two, 2 * two + 1):
            value = dot32(att_ref[b][:, :C], wo_ref[...])
            parts.append(value + own_ref[:, 4 * part + b].reshape(128, C).astype(F32))
        for f in range(16):
            rows = jnp.concatenate([p[8 * f : 8 * f + 8] for p in parts], axis=0)
            mixed_ref[f, 16 * two : 16 * two + 16, :] = rows.astype(BF16)
    for k in range(4):
        other = lax.bitwise_xor(quad, k)
        for f in range(4):
            outs[k][f] = mixed_ref[4 * other + f]


def home_kernel(*refs):
    pieces, out_ref, cells_ref = refs[:8], refs[8], refs[9]
    quad = lax.rem(lax.axis_index("tm"), 4)
    for k in range(4):
        for part in range(2):
            start = pl.multiple_of(64 * lax.bitwise_xor(quad, k) + 32 * part, 32)
            for f in range(4):
                cells_ref[f, pl.ds(start, 32), :] = pieces[4 * part + k][f]
    for f in range(4):
        for row in range(2):
            value = cells_ref[f, row * COLS : (row + 1) * COLS, :].astype(F32)
            out_ref[f, row] = value.T.astype(BF16)


def cost(flops):
    return pl.CostEstimate(flops=flops, bytes_accessed=0, transcendentals=0)


def vmem(count):
    return [pl.BlockSpec(memory_space=pltpu.VMEM)] * count


def body(
    latents, levels, conv_first, emb_weight, conv_second, ln_gain, w_query, w_key, w_value, w_out
):
    size = lax.axis_size("tm")
    latents = jnp.transpose(latents, (0, 1, 3, 2))
    params = pltpu.CompilerParams(vmem_limit_bytes=28 * 2**20)
    halves = jax.ShapeDtypeStruct((1, 2, C, COLS), BF16)
    hbm = pl.BlockSpec(memory_space=pltpu.HBM)
    send = pl.pallas_call(
        pick_kernel,
        out_shape=halves,
        in_specs=[hbm],
        out_specs=pl.BlockSpec(memory_space=pltpu.VMEM),
        scratch_shapes=[pltpu.SemaphoreType.DMA(())],
        compiler_params=params,
        name="pick",
    )(in_hbm(latents))
    got = [lax.ppermute(send, "height", [(0, 1), (1, 0)])]
    first, second, send = pl.pallas_call(
        pack_kernel,
        out_shape=[jax.ShapeDtypeStruct((1024, 3 * C), BF16)] * 2 + [halves],
        in_specs=[hbm] * 3,
        out_specs=vmem(3),
        scratch_shapes=[
            pltpu.VMEM((2, 3, 3, C, C), BF16),
            pltpu.SemaphoreType.DMA((2, 3)),
            pltpu.SemaphoreType.DMA(()),
        ],
        compiler_params=params,
        cost_estimate=cost(1_000_000_000),
        name="pack_weights",
    )(in_hbm(conv_first), in_hbm(conv_second), in_hbm(latents))
    got.append(lax.ppermute(send, "height", [(0, 1), (1, 0)]))
    emb = level_embedding(levels, emb_weight)
    ids = jnp.arange(C) // (C // GROUPS)
    group_map = (ids[:, None] == ids[None, :]).astype(BF16)

    before = []
    for frame in range(2):
        piece = [jax.ShapeDtypeStruct((8, 16, C), BF16)] * 8
        whole = [jax.ShapeDtypeStruct((CELLS, C), F32)]
        pieces = pl.pallas_call(
            functools.partial(block_kernel, frame),
            out_shape=piece if frame else whole,
            in_specs=vmem(6 + frame),
            out_specs=vmem(8 if frame else 1),
            scratch_shapes=[
                pltpu.VMEM((CELLS, C), F32),
                pltpu.VMEM((CELLS, 1024), BF16),
                pltpu.VMEM((CELLS, 960), F32),
                pltpu.VMEM((CELLS, C), F32),
            ],
            compiler_params=params,
            cost_estimate=cost(4_000_000_000),
            name="resblock",
        )(latents, got[frame], first, second, emb, group_map, *before)
        before = pieces

    swaps = [[(i, i ^ k) for i in range(2 * size)] for k in range(8)]
    pieces = [pieces[0]] + [lax.ppermute(pieces[k], AXES, swaps[k]) for k in range(1, 8)]
    def array(*shape):
        return jax.ShapeDtypeStruct(shape, BF16)

    own, *halves = pl.pallas_call(
        gather_kernel,
        out_shape=[array(8, 8, 16, C)] + [array(4, 4, 16, C)] * 4,
        in_specs=vmem(8),
        out_specs=vmem(5),
        compiler_params=params,
        name="by_frame",
    )(*pieces)
    up = [(i, i + 4) for i in range(size - 4) if i // 4 % 2 == 1]
    both = up + [(j, i) for i, j in up]
    far = [lax.ppermute(x, "tm", both) for x in halves[2:]]
    near = [lax.ppermute(x, "tm", [(i, i ^ 4) for i in range(size)]) for x in halves[:2]]
    gain = ln_gain.reshape(1, C)
    query, mine = pl.pallas_call(
        own_kernel,
        out_shape=[array(8, 128, 384), array(8, 128, 768)],
        in_specs=vmem(5),
        out_specs=vmem(2),
        scratch_shapes=[pltpu.VMEM((1024, C), BF16)],
        compiler_params=params,
        cost_estimate=cost(2_000_000_000),
        name="own_frames",
    )(own, gain, w_query, w_key, w_value)
    swaps = [[(i, i ^ k) for i in range(size)] for k in range(4)]
    back = []
    for part in range(2):
        pieces = pl.pallas_call(
            functools.partial(attention_kernel, part),
            out_shape=[array(4, 32, C)] * 4,
            in_specs=vmem(9),
            out_specs=vmem(4),
            scratch_shapes=[
                pltpu.VMEM((512, C), BF16),
                pltpu.VMEM((4, 128, 768), BF16),
                pltpu.VMEM((4, 128, 384), BF16),
                pltpu.VMEM((16, 32, C), BF16),
            ],
            compiler_params=params,
            cost_estimate=cost(2_000_000_000),
            name="window_attention",
        )(own, query, mine, far[part], near[part], gain, w_key, w_value, w_out)
        back += [pieces[0]] + [lax.ppermute(pieces[k], "tm", swaps[k]) for k in range(1, 4)]
    home = pl.pallas_call(
        home_kernel,
        out_shape=jax.ShapeDtypeStruct((4, 2, C, COLS), BF16),
        in_specs=vmem(8),
        out_specs=pl.BlockSpec(memory_space=pltpu.VMEM),
        scratch_shapes=[pltpu.VMEM((4, 256, C), BF16)],
        compiler_params=params,
        name="home",
    )(*back)
    return jnp.transpose(home, (0, 1, 3, 2))


def solution(mesh):
    placed = (P("tm", "height", None, None), P("tm"), P(), P(), P(), P(), P(), P(), P(), P())
    return jax.shard_map(
        body, mesh=mesh, in_specs=placed, out_specs=P("tm", "height", None, None), check_vma=False
    )
```

```python
import functools
import math

import jax
import jax.numpy as jnp
from jax import lax
from jax.experimental import pallas as pl
from jax.experimental.pallas import tpu as pltpu
from jax.sharding import PartitionSpec as P

HEADS = 5
GROUPS = 32
WINDOW = 16
C = 320
MAIN = 256
TAIL = C - MAIN
COLS = 128
CELLS = 512
AXES = ("tm", "height")
F32 = jnp.float32
BF16 = jnp.bfloat16


def dot32(a, b):
    return jnp.dot(a, b, preferred_element_type=F32)


def pick(latents_ref, out_ref, sem, frame):
    there = 1 - lax.axis_index("height")
    return pltpu.make_async_copy(latents_ref.at[pl.ds(2 * there + frame, 1)], out_ref, sem)


def pick_kernel(latents_ref, out_ref, sem):
    copy = pick(latents_ref, out_ref, sem, 0)
    copy.start()
    copy.wait()


def pack_kernel(
    first_ref, second_ref, latents_ref, first_out, second_out, send_out, raw_ref, sems, sem
):
    send = pick(latents_ref, send_out, sem, 1)
    send.start()
    copies = []
    for index, ref in enumerate((first_ref, second_ref)):
        for dy in range(3):
            copies.append(
                pltpu.make_async_copy(ref.at[dy], raw_ref.at[index, dy], sems.at[index, dy])
            )
            copies[-1].start()
    for index, target in enumerate((first_out, second_out)):
        for copy in copies[3 * index : 3 * index + 3]:
            copy.wait()
        source = raw_ref.at[index]
        for dx in range(3):
            for lo, hi, row in ((0, MAIN, dx * MAIN), (MAIN, C, 3 * MAIN + dx * TAIL)):
                rows = slice(row, row + hi - lo)
                for dy in range(3):
                    target[rows, dy * MAIN : (dy + 1) * MAIN] = source[dy, dx, lo:hi, :MAIN]
                tails = [source[dy, dx, lo:hi, MAIN:] for dy in range(3)]
                target[rows, 3 * MAIN :] = jnp.concatenate(tails, axis=1)
        target[3 * C :, :] = jnp.zeros((TAIL, 3 * C), BF16)
    send.wait()


def in_hbm(array):
    return pltpu.with_memory_space_constraint(array, pltpu.HBM)


def level_embedding(levels, emb_weight):
    half = emb_weight.shape[0] // 2
    freqs = jnp.exp(-math.log(10000.0) * jnp.arange(half).astype(jnp.float32) / half)
    angles = levels.astype(jnp.float32)[:, None] * freqs[None, :]
    sinus = jnp.concatenate([jnp.cos(angles), jnp.sin(angles)], axis=1)
    return jnp.dot(
        jax.nn.silu(sinus).astype(jnp.bfloat16), emb_weight, preferred_element_type=jnp.float32
    )


def split3(row):
    first = row.astype(BF16)
    rest = row - first.astype(F32)
    second = rest.astype(BF16)
    return [first, second, (rest - second.astype(F32)).astype(BF16)]


def group_scale(main, tail, group_map):
    total = [jnp.sum(v, axis=0, keepdims=True) for v in (main, tail)]
    square = [jnp.sum(v * v, axis=0, keepdims=True) for v in (main, tail)]
    rows = split3(jnp.concatenate(total, axis=1)) + split3(jnp.concatenate(square, axis=1))
    rows = [r.astype(F32) for r in rows] + [jnp.zeros((2, C), F32)]
    sums = dot32(jnp.concatenate(rows, axis=0).astype(BF16), group_map)
    count = CELLS * (C // GROUPS)
    mean = (sums[0:1] + sums[1:2] + sums[2:3]) / count
    var = (sums[3:4] + sums[4:5] + sums[5:6]) / count - mean * mean
    scale = lax.rsqrt(var + 1e-05)
    return scale, -mean * scale


def silu(u):
    half = 0.5 * u
    return half + half * jnp.tanh(half)


def conv_input(act_ref, main, tail, group_map):
    scale, shift = group_scale(main, tail, group_map)
    column = lax.broadcasted_iota(jnp.int32, (CELLS, 1), 0) % COLS

    def three(value, lo, hi):
        act = silu(value * scale[:, lo:hi] + shift[:, lo:hi])
        before = jnp.where(column == 0, 0.0, pltpu.roll(act, 1, 0))
        after = jnp.where(column == COLS - 1, 0.0, pltpu.roll(act, CELLS - 1, 0))
        return before, act, after

    for index, value in enumerate(three(main, 0, MAIN)):
        act_ref[:, index * MAIN : (index + 1) * MAIN] = value.astype(BF16)
    before, act, after = three(tail, MAIN, C)
    base = 3 * MAIN
    act_ref[:, base : base + 2 * TAIL] = jnp.concatenate([before, act], axis=1).astype(BF16)
    zero = jnp.zeros_like(after)
    act_ref[:, base + 2 * TAIL :] = jnp.concatenate([after, zero], axis=1).astype(BF16)


def conv_rows(act_ref, weight_ref, taps_ref):
    taps_ref[...] = dot32(act_ref[...], weight_ref[...])

    def joined(base, width):
        rows = []
        for row in range(4):
            total = None
            for dy in range(3):
                source = row + dy - 1
                if 0 <= source < 4:
                    piece = taps_ref[
                        source * COLS : (source + 1) * COLS,
                        base + dy * width : base + (dy + 1) * width,
                    ]
                    total = piece if total is None else total + piece
            rows.append(total)
        return jnp.concatenate(rows, axis=0)

    return joined(0, MAIN), joined(3 * MAIN, TAIL)


def block_kernel(
    frame, own_ref, got_ref, first_ref, second_ref, emb_ref, group_ref, *rest
):
    x_ref, act_ref, taps_ref, res_ref = rest[-4:]
    here = lax.axis_index("height")
    ring = 2 * lax.rem(lax.axis_index("tm"), 4) + here
    group_map = group_ref[...]
    for row in range(2):
        for side, raw in ((here, own_ref[2 * here + frame, row]), (1 - here, got_ref[0, row])):
            start = pl.multiple_of((2 * side + row) * COLS, COLS)
            x_ref[pl.ds(start, COLS), :] = raw.astype(F32).T

    def hidden():
        return x_ref[:, :MAIN], x_ref[:, MAIN:]

    conv_input(act_ref, *hidden(), group_map)
    main, tail = conv_rows(act_ref, first_ref, taps_ref)
    emb = emb_ref[pl.ds(2 * here + frame, 1), :]
    conv_input(act_ref, main + emb[:, :MAIN], tail + emb[:, MAIN:], group_map)
    main, tail = conv_rows(act_ref, second_ref, taps_ref)
    old_main, old_tail = hidden()
    target = rest[0] if frame == 0 else res_ref
    target[:, :MAIN] = main + old_main
    target[:, MAIN:] = tail + old_tail
    if frame == 0:
        return
    before_ref, outs = rest[0], rest[1:9]
    for k in range(8):
        other = lax.bitwise_xor(ring, k)
        base = 256 * lax.rem(other, 2) + 32 * lax.div(other, 2)
        for b in range(8):
            rows = pl.ds(pl.multiple_of(base + 128 * (b // 4) + 8 * (b % 4), 8), 8)
            pair = [before_ref[rows, :], res_ref[rows, :]]
            outs[k][b] = jnp.concatenate(pair, axis=0).astype(BF16)


def odd_ring():
    return lax.rem(lax.div(lax.axis_index("tm"), 4), 2)


def gather_kernel(*refs):
    pieces, (own_ref, near_refs, far_refs) = refs[:8], (refs[8], refs[9:11], refs[11:])
    ring = 2 * lax.rem(lax.axis_index("tm"), 4) + lax.axis_index("height")
    odd = odd_ring()
    for k in range(8):
        own_ref[lax.bitwise_xor(ring, k)] = pieces[k][...]
    for part in range(2):
        for j in range(4):
            near_refs[part][j] = own_ref[4 * (1 - odd) + j, 4 * part : 4 * part + 4]
            far_refs[part][j] = own_ref[4 * odd + j, 4 * part : 4 * part + 4]


def layer_norm(value, gain):
    value = value.astype(F32)
    mean = jnp.mean(value, axis=-1, keepdims=True)
    centred = value - mean
    var = jnp.mean(centred * centred, axis=-1, keepdims=True)
    return (centred * lax.rsqrt(var + 1e-05) * gain).astype(BF16)


def keys_values(blocks, gain_ref, wk_ref, wv_ref, norm_ref, kv_ref):
    gain = gain_ref[...]
    rows = blocks[0].shape[0]
    for b, value in enumerate(blocks):
        norm_ref[b * rows : (b + 1) * rows, :] = layer_norm(value, gain)
    each = len(blocks) if rows * len(blocks) <= 512 else 512 // rows
    for b in range(0, len(blocks), each):
        normed = norm_ref[b * rows : (b + each) * rows, :]
        for low, ref in ((0, wk_ref), (384, wv_ref)):
            value = dot32(normed, ref[...]).astype(BF16).reshape(each, rows, C)
            kv_ref[b : b + each, :, low : low + C] = value
            pad = jnp.zeros((each, rows, TAIL), BF16)
            kv_ref[b : b + each, :, low + C : low + 384] = pad


def own_kernel(own_ref, gain_ref, wq_ref, wk_ref, wv_ref, q_ref, kv_ref, norm_ref):
    blocks = [own_ref[:, b].reshape(128, C) for b in range(8)]
    keys_values(blocks, gain_ref, wk_ref, wv_ref, norm_ref, kv_ref)
    for b in range(0, 8, 4):
        value = dot32(norm_ref[128 * b : 128 * b + 512, :], wq_ref[...]) * 0.125
        q_ref[b : b + 4, :, :C] = value.astype(BF16).reshape(4, 128, C)
        q_ref[b : b + 4, :, C:] = jnp.zeros((4, 128, TAIL), BF16)


def attention_kernel(
    part, own_ref, q_ref, mine_ref, one_ref, two_ref, gain_ref, wk_ref, wv_ref, wo_ref, *rest
):
    near_ref, far_ref = one_ref, two_ref
    outs, (norm_ref, kv_ref, att_ref, mixed_ref) = rest[:4], rest[4:]
    tm = lax.axis_index("tm")
    quad = lax.rem(tm, 4)
    base = lax.div(tm, 4) * 16
    odd = odd_ring()
    blocks = [
        jnp.concatenate([r[:, b].reshape(64, C) for r in (near_ref, far_ref)], axis=0)
        for b in range(4)
    ]
    keys_values(blocks, gain_ref, wk_ref, wv_ref, norm_ref, kv_ref)
    row = lax.broadcasted_iota(jnp.int32, (128, 256), 0)
    col = lax.broadcasted_iota(jnp.int32, (128, 256), 1)
    near_at, far_at = 16 - 24 * odd, 24 * odd - 16
    key = col // 8 + jnp.where(col < 64, near_at, jnp.where(col < 128, far_at, -16))
    away = key - row // 8
    keep = (row % 8 == col % 8) & (away >= -(WINDOW // 2)) & (away < WINDOW // 2)
    keep = keep & (base + key >= 0) & (base + key < 4 * lax.axis_size("tm"))
    bias = jnp.where(keep, 0.0, -1e30).astype(F32)
    bias2 = jnp.concatenate([bias, bias], axis=0)
    ones = jnp.ones((256, 128), BF16)
    lane = lax.broadcasted_iota(jnp.int32, (128, 128), 1)

    def keys(b, low):
        full = 4 * part + b
        sides = [kv_ref[b], mine_ref[full]]
        return jnp.concatenate([x[:, low : low + 128] for x in sides], axis=0)

    for first in range(0, 4, 2):
        items = [(b, 128 * pair) for b in (first, first + 1) for pair in range(3)]
        probs = []
        for b, low in items:
            q = q_ref[4 * part + b, :, low : low + 128]
            add = bias
            if low < 256:
                zero = jnp.zeros_like(q)
                q = jnp.concatenate(
                    [jnp.where(lane < 64, q, zero), jnp.where(lane < 64, zero, q)], axis=0
                )
                add = bias2
            score = lax.dot_general(
                q, keys(b, low), (((1,), (1,)), ((), ())), preferred_element_type=F32
            )
            probs.append(jnp.exp(score + add).astype(BF16))
        for (b, low), prob in zip(items, probs):
            mixed = dot32(prob, jnp.concatenate([keys(b, 384 + low), ones], axis=1))
            mixed = mixed[:, :128] / mixed[:, 128:]
            if low < 256:
                mixed = jnp.where(lane < 64, mixed[:128], mixed[128:])
            att_ref[b, :, low : low + 128] = mixed.astype(BF16)
    for two in range(2):
        parts = []
        for b in (2 * two, 2 * two + 1):
            value = dot32(att_ref[b][:, :C], wo_ref[...])
            parts.append(value + own_ref[:, 4 * part + b].reshape(128, C).astype(F32))
        for f in range(16):
            rows = jnp.concatenate([p[8 * f : 8 * f + 8] for p in parts], axis=0)
            mixed_ref[f, 16 * two : 16 * two + 16, :] = rows.astype(BF16)
    for k in range(4):
        other = lax.bitwise_xor(quad, k)
        for f in range(4):
            outs[k][f] = mixed_ref[4 * other + f]


def home_kernel(part, *refs):
    pieces, (out_ref, cells_ref, row_ref, sems) = refs[:4], refs[-4:]
    quad = lax.rem(lax.axis_index("tm"), 4)
    copies = []
    for f in range(4):
        for k in range(4):
            start = pl.multiple_of(32 * lax.bitwise_xor(quad, k), 32)
            cells_ref[f, pl.ds(start, 32), :] = pieces[k][f]
        row_ref[f] = cells_ref[f].astype(F32).T.astype(BF16)
        copies.append(pltpu.make_async_copy(row_ref.at[f], out_ref.at[f, part], sems.at[f]))
        copies[-1].start()
    for copy in copies:
        copy.wait()


def cost(flops):
    return pl.CostEstimate(flops=flops, bytes_accessed=0, transcendentals=0)


def vmem(count):
    return [pl.BlockSpec(memory_space=pltpu.VMEM)] * count


def body(
    latents, levels, conv_first, emb_weight, conv_second, ln_gain, w_query, w_key, w_value, w_out
):
    size = lax.axis_size("tm")
    latents = jnp.transpose(latents, (0, 1, 3, 2))
    params = pltpu.CompilerParams(vmem_limit_bytes=28 * 2**20)
    halves = jax.ShapeDtypeStruct((1, 2, C, COLS), BF16)
    hbm = pl.BlockSpec(memory_space=pltpu.HBM)
    send = pl.pallas_call(
        pick_kernel,
        out_shape=halves,
        in_specs=[hbm],
        out_specs=pl.BlockSpec(memory_space=pltpu.VMEM),
        scratch_shapes=[pltpu.SemaphoreType.DMA(())],
        compiler_params=params,
        name="pick",
    )(in_hbm(latents))
    got = [lax.ppermute(send, "height", [(0, 1), (1, 0)])]
    first, second, send = pl.pallas_call(
        pack_kernel,
        out_shape=[jax.ShapeDtypeStruct((1024, 3 * C), BF16)] * 2 + [halves],
        in_specs=[hbm] * 3,
        out_specs=vmem(3),
        scratch_shapes=[
            pltpu.VMEM((2, 3, 3, C, C), BF16),
            pltpu.SemaphoreType.DMA((2, 3)),
            pltpu.SemaphoreType.DMA(()),
        ],
        compiler_params=params,
        cost_estimate=cost(1_000_000_000),
        name="pack_weights",
    )(in_hbm(conv_first), in_hbm(conv_second), in_hbm(latents))
    got.append(lax.ppermute(send, "height", [(0, 1), (1, 0)]))
    emb = level_embedding(levels, emb_weight)
    ids = jnp.arange(C) // (C // GROUPS)
    group_map = (ids[:, None] == ids[None, :]).astype(BF16)

    before = []
    for frame in range(2):
        piece = [jax.ShapeDtypeStruct((8, 16, C), BF16)] * 8
        whole = [jax.ShapeDtypeStruct((CELLS, C), F32)]
        pieces = pl.pallas_call(
            functools.partial(block_kernel, frame),
            out_shape=piece if frame else whole,
            in_specs=vmem(6 + frame),
            out_specs=vmem(8 if frame else 1),
            scratch_shapes=[
                pltpu.VMEM((CELLS, C), F32),
                pltpu.VMEM((CELLS, 1024), BF16),
                pltpu.VMEM((CELLS, 960), F32),
                pltpu.VMEM((CELLS, C), F32),
            ],
            compiler_params=params,
            cost_estimate=cost(4_000_000_000),
            name="resblock",
        )(latents, got[frame], first, second, emb, group_map, *before)
        before = pieces

    swaps = [[(i, i ^ k) for i in range(2 * size)] for k in range(8)]
    pieces = [pieces[0]] + [lax.ppermute(pieces[k], AXES, swaps[k]) for k in range(1, 8)]
    def array(*shape):
        return jax.ShapeDtypeStruct(shape, BF16)

    own, *halves = pl.pallas_call(
        gather_kernel,
        out_shape=[array(8, 8, 16, C)] + [array(4, 4, 16, C)] * 4,
        in_specs=vmem(8),
        out_specs=vmem(5),
        compiler_params=params,
        name="by_frame",
    )(*pieces)
    up = [(i, i + 4) for i in range(size - 4) if i // 4 % 2 == 1]
    both = up + [(j, i) for i, j in up]
    far = [lax.ppermute(x, "tm", both) for x in halves[2:]]
    near = [lax.ppermute(x, "tm", [(i, i ^ 4) for i in range(size)]) for x in halves[:2]]
    gain = ln_gain.reshape(1, C)
    query, mine = pl.pallas_call(
        own_kernel,
        out_shape=[array(8, 128, 384), array(8, 128, 768)],
        in_specs=vmem(5),
        out_specs=vmem(2),
        scratch_shapes=[pltpu.VMEM((1024, C), BF16)],
        compiler_params=params,
        cost_estimate=cost(2_000_000_000),
        name="own_frames",
    )(own, gain, w_query, w_key, w_value)
    swaps = [[(i, i ^ k) for i in range(size)] for k in range(4)]
    home = []
    for part in range(2):
        halos = [near[part], far[part]]
        pieces = pl.pallas_call(
            functools.partial(attention_kernel, part),
            out_shape=[array(4, 32, C)] * 4,
            in_specs=vmem(9),
            out_specs=vmem(4),
            scratch_shapes=[
                pltpu.VMEM((512, C), BF16),
                pltpu.VMEM((4, 128, 768), BF16),
                pltpu.VMEM((4, 128, 384), BF16),
                pltpu.VMEM((16, 32, C), BF16),
            ],
            compiler_params=params,
            cost_estimate=cost(2_000_000_000),
            name="window_attention",
        )(own, query, mine, *halos, gain, w_key, w_value, w_out)
        back = [pieces[0]] + [lax.ppermute(pieces[k], "tm", swaps[k]) for k in range(1, 4)]
        home = pl.pallas_call(
            functools.partial(home_kernel, part),
            out_shape=array(4, 2, C, COLS),
            in_specs=vmem(4) + [hbm] * part,
            out_specs=hbm,
            input_output_aliases={4: 0} if part else {},
            scratch_shapes=[
                pltpu.VMEM((4, COLS, C), BF16),
                pltpu.VMEM((4, C, COLS), BF16),
                pltpu.SemaphoreType.DMA((4,)),
            ],
            compiler_params=params,
            cost_estimate=cost(1_000_000),
            name="home",
        )(*back, *([home] if part else []))
    return jnp.transpose(home, (0, 1, 3, 2))


def solution(mesh):
    placed = (P("tm", "height", None, None), P("tm"), P(), P(), P(), P(), P(), P(), P(), P())
    return jax.shard_map(
        body, mesh=mesh, in_specs=placed, out_specs=P("tm", "height", None, None), check_vma=False
    )
```

```python
import functools
import math

import jax
import jax.numpy as jnp
from jax import lax
from jax.experimental import pallas as pl
from jax.experimental.pallas import tpu as pltpu
from jax.sharding import PartitionSpec as P

HEADS = 5
GROUPS = 32
WINDOW = 16
C = 320
MAIN = 256
TAIL = C - MAIN
COLS = 128
CELLS = 512
AXES = ("tm", "height")
F32 = jnp.float32
HOME = [0, 2, 3, 1]
ORDER = [0, 1, 3, 4, 5, 6, 7, 2]
BF16 = jnp.bfloat16


def dot32(a, b):
    return jnp.dot(a, b, preferred_element_type=F32)


def pick(latents_ref, out_ref, sem, frame):
    there = 1 - lax.axis_index("height")
    return pltpu.make_async_copy(latents_ref.at[pl.ds(2 * there + frame, 1)], out_ref, sem)


def pick_kernel(latents_ref, out_ref, sem):
    copy = pick(latents_ref, out_ref, sem, 0)
    copy.start()
    copy.wait()


def pack_kernel(
    first_ref, second_ref, latents_ref, first_out, second_out, send_out, raw_ref, sems, sem
):
    send = pick(latents_ref, send_out, sem, 1)
    send.start()
    copies = []
    for index, ref in enumerate((first_ref, second_ref)):
        for dy in range(3):
            copies.append(
                pltpu.make_async_copy(ref.at[dy], raw_ref.at[index, dy], sems.at[index, dy])
            )
            copies[-1].start()
    for index, target in enumerate((first_out, second_out)):
        for copy in copies[3 * index : 3 * index + 3]:
            copy.wait()
        source = raw_ref.at[index]
        for dx in range(3):
            for lo, hi, row in ((0, MAIN, dx * MAIN), (MAIN, C, 3 * MAIN + dx * TAIL)):
                rows = slice(row, row + hi - lo)
                for dy in range(3):
                    target[rows, dy * MAIN : (dy + 1) * MAIN] = source[dy, dx, lo:hi, :MAIN]
                tails = [source[dy, dx, lo:hi, MAIN:] for dy in range(3)]
                target[rows, 3 * MAIN :] = jnp.concatenate(tails, axis=1)
        target[3 * C :, :] = jnp.zeros((TAIL, 3 * C), BF16)
    send.wait()


def in_hbm(array):
    return pltpu.with_memory_space_constraint(array, pltpu.HBM)


def level_embedding(levels, emb_weight):
    half = emb_weight.shape[0] // 2
    freqs = jnp.exp(-math.log(10000.0) * jnp.arange(half).astype(jnp.float32) / half)
    angles = levels.astype(jnp.float32)[:, None] * freqs[None, :]
    sinus = jnp.concatenate([jnp.cos(angles), jnp.sin(angles)], axis=1)
    return jnp.dot(
        jax.nn.silu(sinus).astype(jnp.bfloat16), emb_weight, preferred_element_type=jnp.float32
    )


def split3(row):
    first = row.astype(BF16)
    rest = row - first.astype(F32)
    second = rest.astype(BF16)
    return [first, second, (rest - second.astype(F32)).astype(BF16)]


def group_scale(main, tail, group_map):
    total = [jnp.sum(v, axis=0, keepdims=True) for v in (main, tail)]
    square = [jnp.sum(v * v, axis=0, keepdims=True) for v in (main, tail)]
    rows = split3(jnp.concatenate(total, axis=1)) + split3(jnp.concatenate(square, axis=1))
    rows = [r.astype(F32) for r in rows] + [jnp.zeros((2, C), F32)]
    sums = dot32(jnp.concatenate(rows, axis=0).astype(BF16), group_map)
    count = CELLS * (C // GROUPS)
    mean = (sums[0:1] + sums[1:2] + sums[2:3]) / count
    var = (sums[3:4] + sums[4:5] + sums[5:6]) / count - mean * mean
    scale = lax.rsqrt(var + 1e-05)
    return scale, -mean * scale


def silu(u):
    half = 0.5 * u
    return half + half * jnp.tanh(half)


def conv_input(act_ref, main, tail, group_map):
    scale, shift = group_scale(main, tail, group_map)
    column = lax.broadcasted_iota(jnp.int32, (CELLS, 1), 0) % COLS

    def three(value, lo, hi):
        act = silu(value * scale[:, lo:hi] + shift[:, lo:hi])
        before = jnp.where(column == 0, 0.0, pltpu.roll(act, 1, 0))
        after = jnp.where(column == COLS - 1, 0.0, pltpu.roll(act, CELLS - 1, 0))
        return before, act, after

    for index, value in enumerate(three(main, 0, MAIN)):
        act_ref[:, index * MAIN : (index + 1) * MAIN] = value.astype(BF16)
    before, act, after = three(tail, MAIN, C)
    base = 3 * MAIN
    act_ref[:, base : base + 2 * TAIL] = jnp.concatenate([before, act], axis=1).astype(BF16)
    zero = jnp.zeros_like(after)
    act_ref[:, base + 2 * TAIL :] = jnp.concatenate([after, zero], axis=1).astype(BF16)


def conv_rows(act_ref, weight_ref, taps_ref):
    taps_ref[...] = dot32(act_ref[...], weight_ref[...])

    def joined(base, width):
        rows = []
        for row in range(4):
            total = None
            for dy in range(3):
                source = row + dy - 1
                if 0 <= source < 4:
                    piece = taps_ref[
                        source * COLS : (source + 1) * COLS,
                        base + dy * width : base + (dy + 1) * width,
                    ]
                    total = piece if total is None else total + piece
            rows.append(total)
        return jnp.concatenate(rows, axis=0)

    return joined(0, MAIN), joined(3 * MAIN, TAIL)


def block_kernel(
    frame, own_ref, got_ref, first_ref, second_ref, emb_ref, group_ref, *rest
):
    x_ref, act_ref, taps_ref, res_ref = rest[-4:]
    here = lax.axis_index("height")
    ring = 2 * lax.rem(lax.axis_index("tm"), 4) + here
    group_map = group_ref[...]
    for row in range(2):
        for side, raw in ((here, own_ref[2 * here + frame, row]), (1 - here, got_ref[0, row])):
            start = pl.multiple_of((2 * side + row) * COLS, COLS)
            x_ref[pl.ds(start, COLS), :] = raw.astype(F32).T

    def hidden():
        return x_ref[:, :MAIN], x_ref[:, MAIN:]

    conv_input(act_ref, *hidden(), group_map)
    main, tail = conv_rows(act_ref, first_ref, taps_ref)
    emb = emb_ref[pl.ds(2 * here + frame, 1), :]
    conv_input(act_ref, main + emb[:, :MAIN], tail + emb[:, MAIN:], group_map)
    main, tail = conv_rows(act_ref, second_ref, taps_ref)
    old_main, old_tail = hidden()
    target = rest[0] if frame == 0 else res_ref
    target[:, :MAIN] = main + old_main
    target[:, MAIN:] = tail + old_tail
    if frame == 0:
        return
    before_ref, outs = rest[0], rest[1:9]
    for k in range(8):
        other = lax.bitwise_xor(ring, k)
        base = 256 * lax.rem(other, 2) + 32 * lax.div(other, 2)
        for b in range(8):
            rows = pl.ds(pl.multiple_of(base + 128 * (b // 4) + 8 * (b % 4), 8), 8)
            pair = [before_ref[rows, :], res_ref[rows, :]]
            outs[ORDER.index(k)][b] = jnp.concatenate(pair, axis=0).astype(BF16)


def odd_ring():
    return lax.rem(lax.div(lax.axis_index("tm"), 4), 2)


def gather_kernel(*refs):
    pieces, (own_ref, near_refs, far_refs) = refs[:8], (refs[8], refs[9:11], refs[11:])
    ring = 2 * lax.rem(lax.axis_index("tm"), 4) + lax.axis_index("height")
    odd = odd_ring()
    for k in range(8):
        own_ref[lax.bitwise_xor(ring, ORDER[k])] = pieces[k][...]
    for part in range(2):
        for j in range(4):
            near_refs[part][j] = own_ref[4 * (1 - odd) + j, 4 * part : 4 * part + 4]
            far_refs[part][j] = own_ref[4 * odd + j, 4 * part : 4 * part + 4]


def layer_norm(value, gain):
    value = value.astype(F32)
    mean = jnp.mean(value, axis=-1, keepdims=True)
    centred = value - mean
    var = jnp.mean(centred * centred, axis=-1, keepdims=True)
    return (centred * lax.rsqrt(var + 1e-05) * gain).astype(BF16)


def keys_values(blocks, gain_ref, wk_ref, wv_ref, norm_ref, kv_ref):
    gain = gain_ref[...]
    rows = blocks[0].shape[0]
    for b, value in enumerate(blocks):
        norm_ref[b * rows : (b + 1) * rows, :] = layer_norm(value, gain)
    each = len(blocks) if rows * len(blocks) <= 512 else 512 // rows
    for b in range(0, len(blocks), each):
        normed = norm_ref[b * rows : (b + each) * rows, :]
        for low, ref in ((0, wk_ref), (384, wv_ref)):
            value = dot32(normed, ref[...]).astype(BF16).reshape(each, rows, C)
            kv_ref[b : b + each, :, low : low + C] = value
            pad = jnp.zeros((each, rows, TAIL), BF16)
            kv_ref[b : b + each, :, low + C : low + 384] = pad


def own_kernel(own_ref, gain_ref, wq_ref, wk_ref, wv_ref, q_ref, kv_ref, norm_ref):
    blocks = [own_ref[:, b].reshape(128, C) for b in range(8)]
    keys_values(blocks, gain_ref, wk_ref, wv_ref, norm_ref, kv_ref)
    for b in range(0, 8, 4):
        value = dot32(norm_ref[128 * b : 128 * b + 512, :], wq_ref[...]) * 0.125
        q_ref[b : b + 4, :, :C] = value.astype(BF16).reshape(4, 128, C)
        q_ref[b : b + 4, :, C:] = jnp.zeros((4, 128, TAIL), BF16)


def attention_kernel(
    part, own_ref, q_ref, mine_ref, one_ref, two_ref, gain_ref, wk_ref, wv_ref, wo_ref, *rest
):
    near_ref, far_ref = one_ref, two_ref
    outs, (norm_ref, kv_ref, att_ref, mixed_ref) = rest[:4], rest[4:]
    tm = lax.axis_index("tm")
    quad = lax.rem(tm, 4)
    base = lax.div(tm, 4) * 16
    odd = odd_ring()
    blocks = [
        jnp.concatenate([r[:, b].reshape(64, C) for r in (near_ref, far_ref)], axis=0)
        for b in range(4)
    ]
    keys_values(blocks, gain_ref, wk_ref, wv_ref, norm_ref, kv_ref)
    row = lax.broadcasted_iota(jnp.int32, (128, 256), 0)
    col = lax.broadcasted_iota(jnp.int32, (128, 256), 1)
    near_at, far_at = 16 - 24 * odd, 24 * odd - 16
    key = col // 8 + jnp.where(col < 64, near_at, jnp.where(col < 128, far_at, -16))
    away = key - row // 8
    keep = (row % 8 == col % 8) & (away >= -(WINDOW // 2)) & (away < WINDOW // 2)
    keep = keep & (base + key >= 0) & (base + key < 4 * lax.axis_size("tm"))
    bias = jnp.where(keep, 0.0, -1e30).astype(F32)
    bias2 = jnp.concatenate([bias, bias], axis=0)
    ones = jnp.ones((256, 128), BF16)
    lane = lax.broadcasted_iota(jnp.int32, (128, 128), 1)

    def keys(b, low):
        full = 4 * part + b
        sides = [kv_ref[b], mine_ref[full]]
        return jnp.concatenate([x[:, low : low + 128] for x in sides], axis=0)

    for first in range(0, 4, 2):
        items = [(b, 128 * pair) for b in (first, first + 1) for pair in range(3)]
        probs = []
        for b, low in items:
            q = q_ref[4 * part + b, :, low : low + 128]
            add = bias
            if low < 256:
                zero = jnp.zeros_like(q)
                q = jnp.concatenate(
                    [jnp.where(lane < 64, q, zero), jnp.where(lane < 64, zero, q)], axis=0
                )
                add = bias2
            score = lax.dot_general(
                q, keys(b, low), (((1,), (1,)), ((), ())), preferred_element_type=F32
            )
            probs.append(jnp.exp(score + add).astype(BF16))
        for (b, low), prob in zip(items, probs):
            mixed = dot32(prob, jnp.concatenate([keys(b, 384 + low), ones], axis=1))
            mixed = mixed[:, :128] / mixed[:, 128:]
            if low < 256:
                mixed = jnp.where(lane < 64, mixed[:128], mixed[128:])
            att_ref[b, :, low : low + 128] = mixed.astype(BF16)
    for two in range(2):
        parts = []
        for b in (2 * two, 2 * two + 1):
            value = dot32(att_ref[b][:, :C], wo_ref[...])
            parts.append(value + own_ref[:, 4 * part + b].reshape(128, C).astype(F32))
        for f in range(16):
            rows = jnp.concatenate([p[8 * f : 8 * f + 8] for p in parts], axis=0)
            mixed_ref[f, 16 * two : 16 * two + 16, :] = rows.astype(BF16)
    for k in range(4):
        other = lax.bitwise_xor(quad, k)
        for f in range(4):
            outs[HOME.index(k)][f] = mixed_ref[4 * other + f]


def home_kernel(part, *refs):
    pieces, (out_ref, cells_ref, row_ref, sems) = refs[:4], refs[-4:]
    quad = lax.rem(lax.axis_index("tm"), 4)
    copies = []
    for f in range(4):
        for k in range(4):
            start = pl.multiple_of(32 * lax.bitwise_xor(quad, HOME[k]), 32)
            cells_ref[f, pl.ds(start, 32), :] = pieces[k][f]
        row_ref[f] = cells_ref[f].astype(F32).T.astype(BF16)
        copies.append(pltpu.make_async_copy(row_ref.at[f], out_ref.at[f, part], sems.at[f]))
        copies[-1].start()
    for copy in copies:
        copy.wait()


def cost(flops):
    return pl.CostEstimate(flops=flops, bytes_accessed=0, transcendentals=0)


def vmem(count):
    return [pl.BlockSpec(memory_space=pltpu.VMEM)] * count


def body(
    latents, levels, conv_first, emb_weight, conv_second, ln_gain, w_query, w_key, w_value, w_out
):
    size = lax.axis_size("tm")
    latents = jnp.transpose(latents, (0, 1, 3, 2))
    params = pltpu.CompilerParams(vmem_limit_bytes=28 * 2**20)
    halves = jax.ShapeDtypeStruct((1, 2, C, COLS), BF16)
    hbm = pl.BlockSpec(memory_space=pltpu.HBM)
    send = pl.pallas_call(
        pick_kernel,
        out_shape=halves,
        in_specs=[hbm],
        out_specs=pl.BlockSpec(memory_space=pltpu.VMEM),
        scratch_shapes=[pltpu.SemaphoreType.DMA(())],
        compiler_params=params,
        name="pick",
    )(in_hbm(latents))
    got = [lax.ppermute(send, "height", [(0, 1), (1, 0)])]
    first, second, send = pl.pallas_call(
        pack_kernel,
        out_shape=[jax.ShapeDtypeStruct((1024, 3 * C), BF16)] * 2 + [halves],
        in_specs=[hbm] * 3,
        out_specs=vmem(3),
        scratch_shapes=[
            pltpu.VMEM((2, 3, 3, C, C), BF16),
            pltpu.SemaphoreType.DMA((2, 3)),
            pltpu.SemaphoreType.DMA(()),
        ],
        compiler_params=params,
        cost_estimate=cost(1_000_000_000),
        name="pack_weights",
    )(in_hbm(conv_first), in_hbm(conv_second), in_hbm(latents))
    got.append(lax.ppermute(send, "height", [(0, 1), (1, 0)]))
    emb = level_embedding(levels, emb_weight)
    ids = jnp.arange(C) // (C // GROUPS)
    group_map = (ids[:, None] == ids[None, :]).astype(BF16)

    before = []
    for frame in range(2):
        piece = [jax.ShapeDtypeStruct((8, 16, C), BF16)] * 8
        whole = [jax.ShapeDtypeStruct((CELLS, C), F32)]
        pieces = pl.pallas_call(
            functools.partial(block_kernel, frame),
            out_shape=piece if frame else whole,
            in_specs=vmem(6 + frame),
            out_specs=vmem(8 if frame else 1),
            scratch_shapes=[
                pltpu.VMEM((CELLS, C), F32),
                pltpu.VMEM((CELLS, 1024), BF16),
                pltpu.VMEM((CELLS, 960), F32),
                pltpu.VMEM((CELLS, C), F32),
            ],
            compiler_params=params,
            cost_estimate=cost(4_000_000_000),
            name="resblock",
        )(latents, got[frame], first, second, emb, group_map, *before)
        before = pieces

    swaps = [[(i, i ^ k) for i in range(2 * size)] for k in range(8)]
    pieces = [pieces[0]] + [lax.ppermute(pieces[k], AXES, swaps[ORDER[k]]) for k in range(1, 8)]
    def array(*shape):
        return jax.ShapeDtypeStruct(shape, BF16)

    own, *halves = pl.pallas_call(
        gather_kernel,
        out_shape=[array(8, 8, 16, C)] + [array(4, 4, 16, C)] * 4,
        in_specs=vmem(8),
        out_specs=vmem(5),
        compiler_params=params,
        name="by_frame",
    )(*pieces)
    up = [(i, i + 4) for i in range(size - 4) if i // 4 % 2 == 1]
    both = up + [(j, i) for i, j in up]
    far = [lax.ppermute(x, "tm", both) for x in halves[2:]]
    near = [lax.ppermute(x, "tm", [(i, i ^ 4) for i in range(size)]) for x in halves[:2]]
    gain = ln_gain.reshape(1, C)
    query, mine = pl.pallas_call(
        own_kernel,
        out_shape=[array(8, 128, 384), array(8, 128, 768)],
        in_specs=vmem(5),
        out_specs=vmem(2),
        scratch_shapes=[pltpu.VMEM((1024, C), BF16)],
        compiler_params=params,
        cost_estimate=cost(2_000_000_000),
        name="own_frames",
    )(own, gain, w_query, w_key, w_value)
    swaps = [[(i, i ^ k) for i in range(size)] for k in range(4)]
    home = []
    for part in range(2):
        halos = [near[part], far[part]]
        pieces = pl.pallas_call(
            functools.partial(attention_kernel, part),
            out_shape=[array(4, 32, C)] * 4,
            in_specs=vmem(9),
            out_specs=vmem(4),
            scratch_shapes=[
                pltpu.VMEM((512, C), BF16),
                pltpu.VMEM((4, 128, 768), BF16),
                pltpu.VMEM((4, 128, 384), BF16),
                pltpu.VMEM((16, 32, C), BF16),
            ],
            compiler_params=params,
            cost_estimate=cost(2_000_000_000),
            name="window_attention",
        )(own, query, mine, *halos, gain, w_key, w_value, w_out)
        back = [pieces[0]] + [lax.ppermute(pieces[k], "tm", swaps[HOME[k]]) for k in range(1, 4)]
        home = pl.pallas_call(
            functools.partial(home_kernel, part),
            out_shape=array(4, 2, C, COLS),
            in_specs=vmem(4) + [hbm] * part,
            out_specs=hbm,
            input_output_aliases={4: 0} if part else {},
            scratch_shapes=[
                pltpu.VMEM((4, COLS, C), BF16),
                pltpu.VMEM((4, C, COLS), BF16),
                pltpu.SemaphoreType.DMA((4,)),
            ],
            compiler_params=params,
            cost_estimate=cost(1_000_000),
            name="home",
        )(*back, *([home] if part else []))
    return jnp.transpose(home, (0, 1, 3, 2))


def solution(mesh):
    placed = (P("tm", "height", None, None), P("tm"), P(), P(), P(), P(), P(), P(), P(), P())
    return jax.shard_map(
        body, mesh=mesh, in_specs=placed, out_specs=P("tm", "height", None, None), check_vma=False
    )
```

```python
import functools
import math

import jax
import jax.numpy as jnp
from jax import lax
from jax.experimental import pallas as pl
from jax.experimental.pallas import tpu as pltpu
from jax.sharding import PartitionSpec as P

HEADS = 5
GROUPS = 32
WINDOW = 16
C = 320
MAIN = 256
TAIL = C - MAIN
COLS = 128
CELLS = 512
AXES = ("tm", "height")
F32 = jnp.float32
HOME = [0, 2, 3, 1]
ORDER = [0, 1, 3, 4, 5, 6, 7, 2]
BF16 = jnp.bfloat16


def dot32(a, b):
    return jnp.dot(a, b, preferred_element_type=F32)


def pick(latents_ref, out_ref, sem, frame):
    there = 1 - lax.axis_index("height")
    return pltpu.make_async_copy(latents_ref.at[pl.ds(2 * there + frame, 1)], out_ref, sem)


def pick_kernel(latents_ref, out_ref, sem):
    copy = pick(latents_ref, out_ref, sem, 0)
    copy.start()
    copy.wait()


def pack_kernel(
    first_ref, second_ref, latents_ref, first_out, second_out, send_out, raw_ref, sems, sem
):
    send = pick(latents_ref, send_out, sem, 1)
    send.start()
    copies = []
    for index, ref in enumerate((first_ref, second_ref)):
        for dy in range(3):
            copies.append(
                pltpu.make_async_copy(ref.at[dy], raw_ref.at[index, dy], sems.at[index, dy])
            )
            copies[-1].start()
    for index, target in enumerate((first_out, second_out)):
        for copy in copies[3 * index : 3 * index + 3]:
            copy.wait()
        source = raw_ref.at[index]
        for dx in range(3):
            for lo, hi, row in ((0, MAIN, dx * MAIN), (MAIN, C, 3 * MAIN + dx * TAIL)):
                rows = slice(row, row + hi - lo)
                for dy in range(3):
                    target[rows, dy * MAIN : (dy + 1) * MAIN] = source[dy, dx, lo:hi, :MAIN]
                tails = [source[dy, dx, lo:hi, MAIN:] for dy in range(3)]
                target[rows, 3 * MAIN :] = jnp.concatenate(tails, axis=1)
        target[3 * C :, :] = jnp.zeros((TAIL, 3 * C), BF16)
    send.wait()


def in_hbm(array):
    return pltpu.with_memory_space_constraint(array, pltpu.HBM)


def level_embedding(levels, emb_weight):
    half = emb_weight.shape[0] // 2
    freqs = jnp.exp(-math.log(10000.0) * jnp.arange(half).astype(jnp.float32) / half)
    angles = levels.astype(jnp.float32)[:, None] * freqs[None, :]
    sinus = jnp.concatenate([jnp.cos(angles), jnp.sin(angles)], axis=1)
    return jnp.dot(
        jax.nn.silu(sinus).astype(jnp.bfloat16), emb_weight, preferred_element_type=jnp.float32
    )


def split3(row):
    first = row.astype(BF16)
    rest = row - first.astype(F32)
    second = rest.astype(BF16)
    return [first, second, (rest - second.astype(F32)).astype(BF16)]


def group_scale(main, tail, group_map):
    total = [jnp.sum(v, axis=0, keepdims=True) for v in (main, tail)]
    square = [jnp.sum(v * v, axis=0, keepdims=True) for v in (main, tail)]
    rows = split3(jnp.concatenate(total, axis=1)) + split3(jnp.concatenate(square, axis=1))
    rows = [r.astype(F32) for r in rows] + [jnp.zeros((2, C), F32)]
    sums = dot32(jnp.concatenate(rows, axis=0).astype(BF16), group_map)
    count = CELLS * (C // GROUPS)
    mean = (sums[0:1] + sums[1:2] + sums[2:3]) / count
    var = (sums[3:4] + sums[4:5] + sums[5:6]) / count - mean * mean
    scale = lax.rsqrt(var + 1e-05)
    return scale, -mean * scale


def silu(u):
    half = 0.5 * u
    return half + half * jnp.tanh(half)


def conv_input(act_ref, main, tail, group_map):
    scale, shift = group_scale(main, tail, group_map)
    column = lax.broadcasted_iota(jnp.int32, (CELLS, 1), 0) % COLS

    def three(value, lo, hi):
        act = silu(value * scale[:, lo:hi] + shift[:, lo:hi])
        before = jnp.where(column == 0, 0.0, pltpu.roll(act, 1, 0))
        after = jnp.where(column == COLS - 1, 0.0, pltpu.roll(act, CELLS - 1, 0))
        return before, act, after

    for index, value in enumerate(three(main, 0, MAIN)):
        act_ref[:, index * MAIN : (index + 1) * MAIN] = value.astype(BF16)
    before, act, after = three(tail, MAIN, C)
    base = 3 * MAIN
    act_ref[:, base : base + 2 * TAIL] = jnp.concatenate([before, act], axis=1).astype(BF16)
    zero = jnp.zeros_like(after)
    act_ref[:, base + 2 * TAIL :] = jnp.concatenate([after, zero], axis=1).astype(BF16)


def conv_rows(act_ref, weight_ref, taps_ref):
    taps_ref[...] = dot32(act_ref[...], weight_ref[...])

    def joined(base, width):
        rows = []
        for row in range(4):
            total = None
            for dy in range(3):
                source = row + dy - 1
                if 0 <= source < 4:
                    piece = taps_ref[
                        source * COLS : (source + 1) * COLS,
                        base + dy * width : base + (dy + 1) * width,
                    ]
                    total = piece if total is None else total + piece
            rows.append(total)
        return jnp.concatenate(rows, axis=0)

    return joined(0, MAIN), joined(3 * MAIN, TAIL)


def block_kernel(
    frame, own_ref, got_ref, first_ref, second_ref, emb_ref, group_ref, *rest
):
    x_ref, act_ref, taps_ref, res_ref = rest[-4:]
    here = lax.axis_index("height")
    ring = 2 * lax.rem(lax.axis_index("tm"), 4) + here
    group_map = group_ref[...]
    for row in range(2):
        for side, raw in ((here, own_ref[2 * here + frame, row]), (1 - here, got_ref[0, row])):
            start = pl.multiple_of((2 * side + row) * COLS, COLS)
            x_ref[pl.ds(start, COLS), :] = raw.T.astype(F32)

    def hidden():
        return x_ref[:, :MAIN], x_ref[:, MAIN:]

    conv_input(act_ref, *hidden(), group_map)
    main, tail = conv_rows(act_ref, first_ref, taps_ref)
    emb = emb_ref[pl.ds(2 * here + frame, 1), :]
    conv_input(act_ref, main + emb[:, :MAIN], tail + emb[:, MAIN:], group_map)
    main, tail = conv_rows(act_ref, second_ref, taps_ref)
    old_main, old_tail = hidden()
    target = rest[0] if frame == 0 else res_ref
    target[:, :MAIN] = main + old_main
    target[:, MAIN:] = tail + old_tail
    if frame == 0:
        return
    before_ref, outs = rest[0], rest[1:9]
    for k in range(8):
        other = lax.bitwise_xor(ring, k)
        base = 256 * lax.rem(other, 2) + 32 * lax.div(other, 2)
        for b in range(8):
            rows = pl.ds(pl.multiple_of(base + 128 * (b // 4) + 8 * (b % 4), 8), 8)
            pair = [before_ref[rows, :], res_ref[rows, :]]
            outs[ORDER.index(k)][b] = jnp.concatenate(pair, axis=0).astype(BF16)


def odd_ring():
    return lax.rem(lax.div(lax.axis_index("tm"), 4), 2)


def gather_kernel(*refs):
    pieces, (own_ref, near_refs, far_refs) = refs[:8], (refs[8], refs[9:11], refs[11:])
    ring = 2 * lax.rem(lax.axis_index("tm"), 4) + lax.axis_index("height")
    odd = odd_ring()
    for k in range(8):
        own_ref[lax.bitwise_xor(ring, ORDER[k])] = pieces[k][...]
    for part in range(2):
        for j in range(4):
            near_refs[part][j] = own_ref[4 * (1 - odd) + j, 4 * part : 4 * part + 4]
            far_refs[part][j] = own_ref[4 * odd + j, 4 * part : 4 * part + 4]


def layer_norm(value, gain):
    value = value.astype(F32)
    mean = jnp.mean(value, axis=-1, keepdims=True)
    centred = value - mean
    var = jnp.mean(centred * centred, axis=-1, keepdims=True)
    return (centred * lax.rsqrt(var + 1e-05) * gain).astype(BF16)


def keys_values(blocks, gain_ref, wkv_ref, norm_ref, kv_ref):
    gain = gain_ref[...]
    rows = blocks[0].shape[0]
    for b, value in enumerate(blocks):
        norm_ref[b * rows : (b + 1) * rows, :] = layer_norm(value, gain)
    each = len(blocks) if rows * len(blocks) <= 512 else 512 // rows
    for b in range(0, len(blocks), each):
        normed = norm_ref[b * rows : (b + each) * rows, :]
        kv_ref[b : b + each] = dot32(normed, wkv_ref[...]).astype(BF16).reshape(each, rows, 768)


def window_bias():
    base = lax.div(lax.axis_index("tm"), 4) * 16
    odd = odd_ring()
    row = lax.broadcasted_iota(jnp.int32, (128, 256), 0)
    col = lax.broadcasted_iota(jnp.int32, (128, 256), 1)
    near_at, far_at = 16 - 24 * odd, 24 * odd - 16
    key = col // 8 + jnp.where(col < 64, near_at, jnp.where(col < 128, far_at, -16))
    away = key - row // 8
    keep = (row % 8 == col % 8) & (away >= -(WINDOW // 2)) & (away < WINDOW // 2)
    keep = keep & (base + key >= 0) & (base + key < 4 * lax.axis_size("tm"))
    return jnp.where(keep, 0.0, -1e30).astype(F32)


def own_kernel(
    own_ref, gain_ref, wq_ref, wk_ref, wv_ref, q_ref, kv_ref, wkv_ref, bias_ref, norm_ref
):
    for low, ref in ((0, wk_ref), (384, wv_ref)):
        wkv_ref[:, low : low + C] = ref[...]
        wkv_ref[:, low + C : low + 384] = jnp.zeros((C, TAIL), BF16)
    bias_ref[...] = window_bias()
    blocks = [own_ref[:, b].reshape(128, C) for b in range(8)]
    keys_values(blocks, gain_ref, wkv_ref, norm_ref, kv_ref)
    for b in range(0, 8, 4):
        value = dot32(norm_ref[128 * b : 128 * b + 512, :], wq_ref[...]) * 0.125
        q_ref[b : b + 4, :, :C] = value.astype(BF16).reshape(4, 128, C)
        q_ref[b : b + 4, :, C:] = jnp.zeros((4, 128, TAIL), BF16)


def attention_kernel(
    part, own_ref, q_ref, mine_ref, one_ref, two_ref, gain_ref, wkv_ref, wo_ref, bias_ref, *rest
):
    near_ref, far_ref = one_ref, two_ref
    outs, (norm_ref, kv_ref, att_ref, mixed_ref) = rest[:4], rest[4:]
    quad = lax.rem(lax.axis_index("tm"), 4)
    blocks = [
        jnp.concatenate([r[:, b].reshape(64, C) for r in (near_ref, far_ref)], axis=0)
        for b in range(4)
    ]
    keys_values(blocks, gain_ref, wkv_ref, norm_ref, kv_ref)
    bias = bias_ref[...]
    bias2 = jnp.concatenate([bias, bias], axis=0)
    ones = jnp.ones((256, 128), BF16)
    lane = lax.broadcasted_iota(jnp.int32, (128, 128), 1)

    def keys(b, low):
        full = 4 * part + b
        sides = [kv_ref[b], mine_ref[full]]
        return jnp.concatenate([x[:, low : low + 128] for x in sides], axis=0)

    for first in range(1):
        items = [(b, 128 * pair) for b in range(4) for pair in range(3)]
        probs = []
        for b, low in items:
            q = q_ref[4 * part + b, :, low : low + 128]
            add = bias
            if low < 256:
                zero = jnp.zeros_like(q)
                q = jnp.concatenate(
                    [jnp.where(lane < 64, q, zero), jnp.where(lane < 64, zero, q)], axis=0
                )
                add = bias2
            score = lax.dot_general(
                q, keys(b, low), (((1,), (1,)), ((), ())), preferred_element_type=F32
            )
            probs.append(jnp.exp(score + add).astype(BF16))
        for (b, low), prob in zip(items, probs):
            mixed = dot32(prob, jnp.concatenate([keys(b, 384 + low), ones], axis=1))
            mixed = mixed[:, :128] / mixed[:, 128:]
            if low < 256:
                mixed = jnp.where(lane < 64, mixed[:128], mixed[128:])
            att_ref[b, :, low : low + 128] = mixed.astype(BF16)
    for two in range(2):
        parts = []
        for b in (2 * two, 2 * two + 1):
            value = dot32(att_ref[b][:, :C], wo_ref[...])
            parts.append(value + own_ref[:, 4 * part + b].reshape(128, C).astype(F32))
        for f in range(16):
            rows = jnp.concatenate([p[8 * f : 8 * f + 8] for p in parts], axis=0)
            mixed_ref[f, 16 * two : 16 * two + 16, :] = rows.astype(BF16)
    for k in range(4):
        other = lax.bitwise_xor(quad, k)
        for f in range(4):
            outs[HOME.index(k)][f] = mixed_ref[4 * other + f]


def home_kernel(part, *refs):
    pieces, (out_ref, cells_ref, row_ref, sems) = refs[:4], refs[-4:]
    quad = lax.rem(lax.axis_index("tm"), 4)
    copies = []
    for f in range(4):
        for k in range(4):
            start = pl.multiple_of(32 * lax.bitwise_xor(quad, HOME[k]), 32)
            cells_ref[f, pl.ds(start, 32), :] = pieces[k][f]
        row_ref[f] = cells_ref[f].T
        copies.append(pltpu.make_async_copy(row_ref.at[f], out_ref.at[f, part], sems.at[f]))
        copies[-1].start()
    for copy in copies:
        copy.wait()


def cost(flops):
    return pl.CostEstimate(flops=flops, bytes_accessed=0, transcendentals=0)


def vmem(count):
    return [pl.BlockSpec(memory_space=pltpu.VMEM)] * count


def body(
    latents, levels, conv_first, emb_weight, conv_second, ln_gain, w_query, w_key, w_value, w_out
):
    size = lax.axis_size("tm")
    latents = jnp.transpose(latents, (0, 1, 3, 2))
    params = pltpu.CompilerParams(vmem_limit_bytes=28 * 2**20)
    halves = jax.ShapeDtypeStruct((1, 2, C, COLS), BF16)
    hbm = pl.BlockSpec(memory_space=pltpu.HBM)
    send = pl.pallas_call(
        pick_kernel,
        out_shape=halves,
        in_specs=[hbm],
        out_specs=pl.BlockSpec(memory_space=pltpu.VMEM),
        scratch_shapes=[pltpu.SemaphoreType.DMA(())],
        compiler_params=params,
        name="pick",
    )(in_hbm(latents))
    got = [lax.ppermute(send, "height", [(0, 1), (1, 0)])]
    first, second, send = pl.pallas_call(
        pack_kernel,
        out_shape=[jax.ShapeDtypeStruct((1024, 3 * C), BF16)] * 2 + [halves],
        in_specs=[hbm] * 3,
        out_specs=vmem(3),
        scratch_shapes=[
            pltpu.VMEM((2, 3, 3, C, C), BF16),
            pltpu.SemaphoreType.DMA((2, 3)),
            pltpu.SemaphoreType.DMA(()),
        ],
        compiler_params=params,
        cost_estimate=cost(1_000_000_000),
        name="pack_weights",
    )(in_hbm(conv_first), in_hbm(conv_second), in_hbm(latents))
    got.append(lax.ppermute(send, "height", [(0, 1), (1, 0)]))
    emb = level_embedding(levels, emb_weight)
    ids = jnp.arange(C) // (C // GROUPS)
    group_map = (ids[:, None] == ids[None, :]).astype(BF16)

    before = []
    for frame in range(2):
        piece = [jax.ShapeDtypeStruct((8, 16, C), BF16)] * 8
        whole = [jax.ShapeDtypeStruct((CELLS, C), F32)]
        pieces = pl.pallas_call(
            functools.partial(block_kernel, frame),
            out_shape=piece if frame else whole,
            in_specs=vmem(6 + frame),
            out_specs=vmem(8 if frame else 1),
            scratch_shapes=[
                pltpu.VMEM((CELLS, C), F32),
                pltpu.VMEM((CELLS, 1024), BF16),
                pltpu.VMEM((CELLS, 960), F32),
                pltpu.VMEM((CELLS, C), F32),
            ],
            compiler_params=params,
            cost_estimate=cost(4_000_000_000),
            name="resblock",
        )(latents, got[frame], first, second, emb, group_map, *before)
        before = pieces

    swaps = [[(i, i ^ k) for i in range(2 * size)] for k in range(8)]
    pieces = [pieces[0]] + [lax.ppermute(pieces[k], AXES, swaps[ORDER[k]]) for k in range(1, 8)]
    def array(*shape):
        return jax.ShapeDtypeStruct(shape, BF16)

    own, *halves = pl.pallas_call(
        gather_kernel,
        out_shape=[array(8, 8, 16, C)] + [array(4, 4, 16, C)] * 4,
        in_specs=vmem(8),
        out_specs=vmem(5),
        compiler_params=params,
        name="by_frame",
    )(*pieces)
    up = [(i, i + 4) for i in range(size - 4) if i // 4 % 2 == 1]
    both = up + [(j, i) for i, j in up]
    far = [lax.ppermute(x, "tm", both) for x in halves[2:]]
    near = [lax.ppermute(x, "tm", [(i, i ^ 4) for i in range(size)]) for x in halves[:2]]
    gain = ln_gain.reshape(1, C)
    query, mine, w_both, bias = pl.pallas_call(
        own_kernel,
        out_shape=[
            array(8, 128, 384),
            array(8, 128, 768),
            array(C, 768),
            jax.ShapeDtypeStruct((128, 256), F32),
        ],
        in_specs=vmem(5),
        out_specs=vmem(4),
        scratch_shapes=[pltpu.VMEM((1024, C), BF16)],
        compiler_params=params,
        cost_estimate=cost(2_000_000_000),
        name="own_frames",
    )(own, gain, w_query, w_key, w_value)
    swaps = [[(i, i ^ k) for i in range(size)] for k in range(4)]
    home = []
    for part in range(2):
        halos = [near[part], far[part]]
        pieces = pl.pallas_call(
            functools.partial(attention_kernel, part),
            out_shape=[array(4, 32, C)] * 4,
            in_specs=vmem(9),
            out_specs=vmem(4),
            scratch_shapes=[
                pltpu.VMEM((512, C), BF16),
                pltpu.VMEM((4, 128, 768), BF16),
                pltpu.VMEM((4, 128, 384), BF16),
                pltpu.VMEM((16, 32, C), BF16),
            ],
            compiler_params=params,
            cost_estimate=cost(2_000_000_000),
            name="window_attention",
        )(own, query, mine, *halos, gain, w_both, w_out, bias)
        back = [pieces[0]] + [lax.ppermute(pieces[k], "tm", swaps[HOME[k]]) for k in range(1, 4)]
        home = pl.pallas_call(
            functools.partial(home_kernel, part),
            out_shape=array(4, 2, C, COLS),
            in_specs=vmem(4) + [hbm] * part,
            out_specs=hbm,
            input_output_aliases={4: 0} if part else {},
            scratch_shapes=[
                pltpu.VMEM((4, COLS, C), BF16),
                pltpu.VMEM((4, C, COLS), BF16),
                pltpu.SemaphoreType.DMA((4,)),
            ],
            compiler_params=params,
            cost_estimate=cost(1_000_000),
            name="home",
        )(*back, *([home] if part else []))
    return jnp.transpose(home, (0, 1, 3, 2))


def solution(mesh):
    placed = (P("tm", "height", None, None), P("tm"), P(), P(), P(), P(), P(), P(), P(), P())
    return jax.shard_map(
        body, mesh=mesh, in_specs=placed, out_specs=P("tm", "height", None, None), check_vma=False
    )
```

```python
import functools
import math

import jax
import jax.numpy as jnp
from jax import lax
from jax.experimental import pallas as pl
from jax.experimental.pallas import tpu as pltpu
from jax.sharding import PartitionSpec as P

HEADS = 5
GROUPS = 32
WINDOW = 16
C = 320
MAIN = 256
TAIL = C - MAIN
COLS = 128
CELLS = 512
AXES = ("tm", "height")
F32 = jnp.float32
HOME = [0, 2, 3, 1]
ORDER = [0, 3, 1, 4, 5, 6, 7, 2]
BF16 = jnp.bfloat16


def dot32(a, b):
    return jnp.dot(a, b, preferred_element_type=F32)


def pick(latents_ref, out_ref, sem, frame):
    there = 1 - lax.axis_index("height")
    return pltpu.make_async_copy(latents_ref.at[pl.ds(2 * there + frame, 1)], out_ref, sem)


def pick_kernel(latents_ref, out_ref, sem):
    copy = pick(latents_ref, out_ref, sem, 0)
    copy.start()
    copy.wait()


def pack_kernel(
    first_ref, second_ref, latents_ref, first_out, second_out, send_out, raw_ref, sems, sem
):
    send = pick(latents_ref, send_out, sem, 1)
    send.start()
    copies = []
    for index, ref in enumerate((first_ref, second_ref)):
        for dy in range(3):
            copies.append(
                pltpu.make_async_copy(ref.at[dy], raw_ref.at[index, dy], sems.at[index, dy])
            )
            copies[-1].start()
    for index, target in enumerate((first_out, second_out)):
        for copy in copies[3 * index : 3 * index + 3]:
            copy.wait()
        source = raw_ref.at[index]
        for dx in range(3):
            for lo, hi, row in ((0, MAIN, dx * MAIN), (MAIN, C, 3 * MAIN + dx * TAIL)):
                rows = slice(row, row + hi - lo)
                for dy in range(3):
                    target[rows, dy * MAIN : (dy + 1) * MAIN] = source[dy, dx, lo:hi, :MAIN]
                tails = [source[dy, dx, lo:hi, MAIN:] for dy in range(3)]
                target[rows, 3 * MAIN :] = jnp.concatenate(tails, axis=1)
        target[3 * C :, :] = jnp.zeros((TAIL, 3 * C), BF16)
    send.wait()


def in_hbm(array):
    return pltpu.with_memory_space_constraint(array, pltpu.HBM)


def level_embedding(levels, emb_weight):
    half = emb_weight.shape[0] // 2
    freqs = jnp.exp(-math.log(10000.0) * jnp.arange(half).astype(jnp.float32) / half)
    angles = levels.astype(jnp.float32)[:, None] * freqs[None, :]
    sinus = jnp.concatenate([jnp.cos(angles), jnp.sin(angles)], axis=1)
    return jnp.dot(
        jax.nn.silu(sinus).astype(jnp.bfloat16), emb_weight, preferred_element_type=jnp.float32
    )


def split3(row):
    first = row.astype(BF16)
    rest = row - first.astype(F32)
    second = rest.astype(BF16)
    return [first, second, (rest - second.astype(F32)).astype(BF16)]


def group_scale(main, tail, group_map):
    total = [jnp.sum(v, axis=0, keepdims=True) for v in (main, tail)]
    square = [jnp.sum(v * v, axis=0, keepdims=True) for v in (main, tail)]
    rows = split3(jnp.concatenate(total, axis=1)) + split3(jnp.concatenate(square, axis=1))
    rows = [r.astype(F32) for r in rows] + [jnp.zeros((2, C), F32)]
    sums = dot32(jnp.concatenate(rows, axis=0).astype(BF16), group_map)
    count = CELLS * (C // GROUPS)
    mean = (sums[0:1] + sums[1:2] + sums[2:3]) / count
    var = (sums[3:4] + sums[4:5] + sums[5:6]) / count - mean * mean
    scale = lax.rsqrt(var + 1e-05)
    return scale, -mean * scale


def silu(u):
    half = 0.5 * u
    return half + half * jnp.tanh(half)


def conv_input(act_ref, main, tail, group_map):
    scale, shift = group_scale(main, tail, group_map)
    column = lax.broadcasted_iota(jnp.int32, (CELLS, 1), 0) % COLS

    def three(value, lo, hi):
        act = silu(value * scale[:, lo:hi] + shift[:, lo:hi])
        before = jnp.where(column == 0, 0.0, pltpu.roll(act, 1, 0))
        after = jnp.where(column == COLS - 1, 0.0, pltpu.roll(act, CELLS - 1, 0))
        return before, act, after

    for index, value in enumerate(three(main, 0, MAIN)):
        act_ref[:, index * MAIN : (index + 1) * MAIN] = value.astype(BF16)
    before, act, after = three(tail, MAIN, C)
    base = 3 * MAIN
    act_ref[:, base : base + 2 * TAIL] = jnp.concatenate([before, act], axis=1).astype(BF16)
    zero = jnp.zeros_like(after)
    act_ref[:, base + 2 * TAIL :] = jnp.concatenate([after, zero], axis=1).astype(BF16)


def conv_rows(act_ref, weight_ref, taps_ref):
    taps_ref[...] = dot32(act_ref[...], weight_ref[...])

    def joined(base, width):
        rows = []
        for row in range(4):
            total = None
            for dy in range(3):
                source = row + dy - 1
                if 0 <= source < 4:
                    piece = taps_ref[
                        source * COLS : (source + 1) * COLS,
                        base + dy * width : base + (dy + 1) * width,
                    ]
                    total = piece if total is None else total + piece
            rows.append(total)
        return jnp.concatenate(rows, axis=0)

    return joined(0, MAIN), joined(3 * MAIN, TAIL)


def block_kernel(
    frame, own_ref, got_ref, first_ref, second_ref, emb_ref, group_ref, *rest
):
    x_ref, act_ref, taps_ref, res_ref = rest[-4:]
    here = lax.axis_index("height")
    ring = 2 * lax.rem(lax.axis_index("tm"), 4) + here
    group_map = group_ref[...]
    for row in range(2):
        for side, raw in ((here, own_ref[2 * here + frame, row]), (1 - here, got_ref[0, row])):
            start = pl.multiple_of((2 * side + row) * COLS, COLS)
            x_ref[pl.ds(start, COLS), :] = raw.T.astype(F32)

    def hidden():
        return x_ref[:, :MAIN], x_ref[:, MAIN:]

    conv_input(act_ref, *hidden(), group_map)
    main, tail = conv_rows(act_ref, first_ref, taps_ref)
    emb = emb_ref[pl.ds(2 * here + frame, 1), :]
    conv_input(act_ref, main + emb[:, :MAIN], tail + emb[:, MAIN:], group_map)
    main, tail = conv_rows(act_ref, second_ref, taps_ref)
    old_main, old_tail = hidden()
    target = rest[0] if frame == 0 else res_ref
    target[:, :MAIN] = main + old_main
    target[:, MAIN:] = tail + old_tail
    if frame == 0:
        return
    before_ref, outs = rest[0], rest[1:9]
    for k in range(8):
        other = lax.bitwise_xor(ring, k)
        base = 256 * lax.rem(other, 2) + 32 * lax.div(other, 2)
        for b in range(8):
            rows = pl.ds(pl.multiple_of(base + 128 * (b // 4) + 8 * (b % 4), 8), 8)
            pair = [before_ref[rows, :], res_ref[rows, :]]
            outs[ORDER.index(k)][b] = jnp.concatenate(pair, axis=0).astype(BF16)


def odd_ring():
    return lax.rem(lax.div(lax.axis_index("tm"), 4), 2)


def gather_kernel(*refs):
    pieces, (own_ref, near_refs, far_refs) = refs[:8], (refs[8], refs[9:11], refs[11:])
    ring = 2 * lax.rem(lax.axis_index("tm"), 4) + lax.axis_index("height")
    odd = odd_ring()
    for k in range(8):
        own_ref[lax.bitwise_xor(ring, ORDER[k])] = pieces[k][...]
    for part in range(2):
        for j in range(4):
            near_refs[part][j] = own_ref[4 * (1 - odd) + j, 4 * part : 4 * part + 4]
            far_refs[part][j] = own_ref[4 * odd + j, 4 * part : 4 * part + 4]


def layer_norm(value, gain):
    value = value.astype(F32)
    mean = jnp.mean(value, axis=-1, keepdims=True)
    centred = value - mean
    var = jnp.mean(centred * centred, axis=-1, keepdims=True)
    return (centred * lax.rsqrt(var + 1e-05) * gain).astype(BF16)


def keys_values(blocks, gain_ref, wkv_ref, norm_ref, kv_ref):
    gain = gain_ref[...]
    rows = blocks[0].shape[0]
    for b, value in enumerate(blocks):
        norm_ref[b * rows : (b + 1) * rows, :] = layer_norm(value, gain)
    each = len(blocks) if rows * len(blocks) <= 512 else 512 // rows
    for b in range(0, len(blocks), each):
        normed = norm_ref[b * rows : (b + each) * rows, :]
        kv_ref[b : b + each] = dot32(normed, wkv_ref[...]).astype(BF16).reshape(each, rows, 768)


def window_bias():
    base = lax.div(lax.axis_index("tm"), 4) * 16
    odd = odd_ring()
    row = lax.broadcasted_iota(jnp.int32, (128, 256), 0)
    col = lax.broadcasted_iota(jnp.int32, (128, 256), 1)
    near_at, far_at = 16 - 24 * odd, 24 * odd - 16
    key = col // 8 + jnp.where(col < 64, near_at, jnp.where(col < 128, far_at, -16))
    away = key - row // 8
    keep = (row % 8 == col % 8) & (away >= -(WINDOW // 2)) & (away < WINDOW // 2)
    keep = keep & (base + key >= 0) & (base + key < 4 * lax.axis_size("tm"))
    return jnp.where(keep, 0.0, -1e30).astype(F32)


def own_kernel(
    own_ref, gain_ref, wq_ref, wk_ref, wv_ref, q_ref, kv_ref, wkv_ref, bias_ref, norm_ref
):
    for low, ref in ((0, wk_ref), (384, wv_ref)):
        wkv_ref[:, low : low + C] = ref[...]
        wkv_ref[:, low + C : low + 384] = jnp.zeros((C, TAIL), BF16)
    bias_ref[...] = window_bias()
    blocks = [own_ref[:, b].reshape(128, C) for b in range(8)]
    keys_values(blocks, gain_ref, wkv_ref, norm_ref, kv_ref)
    for b in range(0, 8, 4):
        value = dot32(norm_ref[128 * b : 128 * b + 512, :], wq_ref[...]) * 0.125
        q_ref[b : b + 4, :, :C] = value.astype(BF16).reshape(4, 128, C)
        q_ref[b : b + 4, :, C:] = jnp.zeros((4, 128, TAIL), BF16)


def attention_kernel(
    part, own_ref, q_ref, mine_ref, one_ref, two_ref, gain_ref, wkv_ref, wo_ref, bias_ref, *rest
):
    near_ref, far_ref = one_ref, two_ref
    outs, (norm_ref, kv_ref, att_ref, mixed_ref) = rest[:4], rest[4:]
    quad = lax.rem(lax.axis_index("tm"), 4)
    blocks = [
        jnp.concatenate([r[:, b].reshape(64, C) for r in (near_ref, far_ref)], axis=0)
        for b in range(4)
    ]
    keys_values(blocks, gain_ref, wkv_ref, norm_ref, kv_ref)
    bias = bias_ref[...]
    bias2 = jnp.concatenate([bias, bias], axis=0)
    ones = jnp.ones((256, 128), BF16)
    lane = lax.broadcasted_iota(jnp.int32, (128, 128), 1)

    def keys(b, low):
        full = 4 * part + b
        sides = [kv_ref[b], mine_ref[full]]
        return jnp.concatenate([x[:, low : low + 128] for x in sides], axis=0)

    for first in range(1):
        items = [(b, 128 * pair) for b in range(4) for pair in range(3)]
        probs = []
        for b, low in items:
            q = q_ref[4 * part + b, :, low : low + 128]
            add = bias
            if low < 256:
                zero = jnp.zeros_like(q)
                q = jnp.concatenate(
                    [jnp.where(lane < 64, q, zero), jnp.where(lane < 64, zero, q)], axis=0
                )
                add = bias2
            score = lax.dot_general(
                q, keys(b, low), (((1,), (1,)), ((), ())), preferred_element_type=F32
            )
            probs.append(jnp.exp(score + add).astype(BF16))
        for (b, low), prob in zip(items, probs):
            mixed = dot32(prob, jnp.concatenate([keys(b, 384 + low), ones], axis=1))
            mixed = mixed[:, :128] / mixed[:, 128:]
            if low < 256:
                mixed = jnp.where(lane < 64, mixed[:128], mixed[128:])
            att_ref[b, :, low : low + 128] = mixed.astype(BF16)
    for two in range(2):
        parts = []
        for b in (2 * two, 2 * two + 1):
            value = dot32(att_ref[b][:, :C], wo_ref[...])
            parts.append(value + own_ref[:, 4 * part + b].reshape(128, C).astype(F32))
        for f in range(16):
            rows = jnp.concatenate([p[8 * f : 8 * f + 8] for p in parts], axis=0)
            mixed_ref[f, 16 * two : 16 * two + 16, :] = rows.astype(BF16)
    for k in range(4):
        other = lax.bitwise_xor(quad, k)
        for f in range(4):
            outs[HOME.index(k)][f] = mixed_ref[4 * other + f]


def home_kernel(part, *refs):
    pieces, (out_ref, cells_ref, row_ref, sems) = refs[:4], refs[-4:]
    quad = lax.rem(lax.axis_index("tm"), 4)
    copies = []
    for f in range(4):
        for k in range(4):
            start = pl.multiple_of(32 * lax.bitwise_xor(quad, HOME[k]), 32)
            cells_ref[f, pl.ds(start, 32), :] = pieces[k][f]
        row_ref[f] = cells_ref[f].T
        copies.append(pltpu.make_async_copy(row_ref.at[f], out_ref.at[f, part], sems.at[f]))
        copies[-1].start()
    for copy in copies:
        copy.wait()


def cost(flops):
    return pl.CostEstimate(flops=flops, bytes_accessed=0, transcendentals=0)


def vmem(count):
    return [pl.BlockSpec(memory_space=pltpu.VMEM)] * count


def body(
    latents, levels, conv_first, emb_weight, conv_second, ln_gain, w_query, w_key, w_value, w_out
):
    size = lax.axis_size("tm")
    latents = jnp.transpose(latents, (0, 1, 3, 2))
    params = pltpu.CompilerParams(vmem_limit_bytes=28 * 2**20)
    halves = jax.ShapeDtypeStruct((1, 2, C, COLS), BF16)
    hbm = pl.BlockSpec(memory_space=pltpu.HBM)
    send = pl.pallas_call(
        pick_kernel,
        out_shape=halves,
        in_specs=[hbm],
        out_specs=pl.BlockSpec(memory_space=pltpu.VMEM),
        scratch_shapes=[pltpu.SemaphoreType.DMA(())],
        compiler_params=params,
        name="pick",
    )(in_hbm(latents))
    got = [lax.ppermute(send, "height", [(0, 1), (1, 0)])]
    first, second, send = pl.pallas_call(
        pack_kernel,
        out_shape=[jax.ShapeDtypeStruct((1024, 3 * C), BF16)] * 2 + [halves],
        in_specs=[hbm] * 3,
        out_specs=vmem(3),
        scratch_shapes=[
            pltpu.VMEM((2, 3, 3, C, C), BF16),
            pltpu.SemaphoreType.DMA((2, 3)),
            pltpu.SemaphoreType.DMA(()),
        ],
        compiler_params=params,
        cost_estimate=cost(1_000_000_000),
        name="pack_weights",
    )(in_hbm(conv_first), in_hbm(conv_second), in_hbm(latents))
    got.append(lax.ppermute(send, "height", [(0, 1), (1, 0)]))
    emb = level_embedding(levels, emb_weight)
    ids = jnp.arange(C) // (C // GROUPS)
    group_map = (ids[:, None] == ids[None, :]).astype(BF16)

    before = []
    for frame in range(2):
        piece = [jax.ShapeDtypeStruct((8, 16, C), BF16)] * 8
        whole = [jax.ShapeDtypeStruct((CELLS, C), F32)]
        pieces = pl.pallas_call(
            functools.partial(block_kernel, frame),
            out_shape=piece if frame else whole,
            in_specs=vmem(6 + frame),
            out_specs=vmem(8 if frame else 1),
            scratch_shapes=[
                pltpu.VMEM((CELLS, C), F32),
                pltpu.VMEM((CELLS, 1024), BF16),
                pltpu.VMEM((CELLS, 960), F32),
                pltpu.VMEM((CELLS, C), F32),
            ],
            compiler_params=params,
            cost_estimate=cost(4_000_000_000),
            name="resblock",
        )(latents, got[frame], first, second, emb, group_map, *before)
        before = pieces

    swaps = [[(i, i ^ k) for i in range(2 * size)] for k in range(8)]
    pieces = [pieces[0]] + [lax.ppermute(pieces[k], AXES, swaps[ORDER[k]]) for k in range(1, 8)]
    def array(*shape):
        return jax.ShapeDtypeStruct(shape, BF16)

    own, *halves = pl.pallas_call(
        gather_kernel,
        out_shape=[array(8, 8, 16, C)] + [array(4, 4, 16, C)] * 4,
        in_specs=vmem(8),
        out_specs=vmem(5),
        compiler_params=params,
        name="by_frame",
    )(*pieces)
    up = [(i, i + 4) for i in range(size - 4) if i // 4 % 2 == 1]
    both = up + [(j, i) for i, j in up]
    far = [lax.ppermute(x, "tm", both) for x in halves[2:]]
    near = [lax.ppermute(x, "tm", [(i, i ^ 4) for i in range(size)]) for x in halves[:2]]
    gain = ln_gain.reshape(1, C)
    query, mine, w_both, bias = pl.pallas_call(
        own_kernel,
        out_shape=[
            array(8, 128, 384),
            array(8, 128, 768),
            array(C, 768),
            jax.ShapeDtypeStruct((128, 256), F32),
        ],
        in_specs=vmem(5),
        out_specs=vmem(4),
        scratch_shapes=[pltpu.VMEM((1024, C), BF16)],
        compiler_params=params,
        cost_estimate=cost(2_000_000_000),
        name="own_frames",
    )(own, gain, w_query, w_key, w_value)
    swaps = [[(i, i ^ k) for i in range(size)] for k in range(4)]
    home = []
    for part in range(2):
        halos = [near[part], far[part]]
        pieces = pl.pallas_call(
            functools.partial(attention_kernel, part),
            out_shape=[array(4, 32, C)] * 4,
            in_specs=vmem(9),
            out_specs=vmem(4),
            scratch_shapes=[
                pltpu.VMEM((512, C), BF16),
                pltpu.VMEM((4, 128, 768), BF16),
                pltpu.VMEM((4, 128, 384), BF16),
                pltpu.VMEM((16, 32, C), BF16),
            ],
            compiler_params=params,
            cost_estimate=cost(2_000_000_000),
            name="window_attention",
        )(own, query, mine, *halos, gain, w_both, w_out, bias)
        back = [pieces[0]] + [lax.ppermute(pieces[k], "tm", swaps[HOME[k]]) for k in range(1, 4)]
        home = pl.pallas_call(
            functools.partial(home_kernel, part),
            out_shape=array(4, 2, C, COLS),
            in_specs=vmem(4) + [hbm] * part,
            out_specs=hbm,
            input_output_aliases={4: 0} if part else {},
            scratch_shapes=[
                pltpu.VMEM((4, COLS, C), BF16),
                pltpu.VMEM((4, C, COLS), BF16),
                pltpu.SemaphoreType.DMA((4,)),
            ],
            compiler_params=params,
            cost_estimate=cost(1_000_000),
            name="home",
        )(*back, *([home] if part else []))
    return jnp.transpose(home, (0, 1, 3, 2))


def solution(mesh):
    placed = (P("tm", "height", None, None), P("tm"), P(), P(), P(), P(), P(), P(), P(), P())
    return jax.shard_map(
        body, mesh=mesh, in_specs=placed, out_specs=P("tm", "height", None, None), check_vma=False
    )
```
